256 devices in a mesh: col: 8 (over z_hi, x), row: 32 (over z_lo, y, core).
Axes of the slice: x: 4, y: 4, z: 8 (z_hi: 2, z_lo: 4; z = z_hi * 4 + z_lo), core: 2. Of those that a mesh axis runs over, the one named last changes fastest.
Arguments:
- trial_states: float32 [16, 2, 131072], P('col', None, 'row'), may hold values from -6 to 6
- resident: bfloat16 [128, 2, 131072], P('col', None, 'row'), may hold values from -6 to 6
- potential: float32 [128, 128, 128], P('row'), may hold values from -1 to 2
- stick_columns: int32 [4096], P('row'), may hold values from 0 to 16383, as said below
- gvector_cells: int32 [131072], P('row'), may hold values from 0 to 16383, as said below
- slab_owner: int32 [32], replicated, may hold values from 0 to 31, each once
- panel_owner: int32 [8], replicated, may hold values from 0 to 7, as said below
- rotation: bfloat16 [128, 128], P(None, 'col'), may hold values from -0.5 to 0.5
Outputs:
- applied: float32 [16, 2, 131072], P('col', None, 'row')
- rotated: bfloat16 [128, 2, 131072], P('col', None, 'row')
The draws below stay inside these ranges and needn't reach their ends.
Inputs may be any that keep to these rules, and one draw needn't show every extreme that they name: `stick_columns`: the 4096 entries are distinct grid columns. `gvector_cells`: within each row's block of 4096 entries the cells are distinct. `panel_owner`: every column group owns at least one panel.
All inputs are finite; a program needn't handle non-finite values.
Results may differ from the reference program's by a relative error of at most 0.0034.
Values may be sent and summed in bfloat16 or wider, within the bound.
A program may use at most 128 MiB of HBM per device.

```python
import jax
import jax.numpy as jnp
from jax import lax

NG = 128
STK_DEV = 128
RES_DEV = 16
PANELS = 8
NPW_DEV = 4096
NZD = 4
STICKS = 4096
NPW = 131072
TRIALS = 16
RES = 128
N_COL = 8
N_ROW = 32


def draw_stick_columns(key, part):
    top_column = NG * NG - 1
    middle = jax.random.permutation(jax.random.fold_in(key, 1), NG * NG - 2)[:STICKS - 2] + 1
    joined = jnp.concatenate([jnp.array([0, top_column], jnp.int32), middle.astype(jnp.int32)])
    order = jax.random.permutation(jax.random.fold_in(key, 2), STICKS)
    return joined[order].astype(jnp.int32)


def draw_gvector_cells(key, part):

    def one_row(row_number):
        return jax.random.permutation(jax.random.fold_in(key, row_number), STK_DEV * NG)[:NPW_DEV]
    return jax.vmap(one_row)(jnp.arange(STICKS // STK_DEV)).reshape(-1).astype(jnp.int32)


def draw_panel_owner(key, part):
    key = jax.random.fold_in(key, 7)
    groups = jax.random.permutation(jax.random.fold_in(key, 1), N_COL).astype(jnp.int32)
    tiled = groups[jnp.arange(PANELS) % N_COL]
    return jax.random.permutation(jax.random.fold_in(key, 2), tiled).astype(jnp.int32)


def block_scale(rng, extent, pieces, smallest, top_value):
    loudness, own = 1.0, jax.random.fold_in(rng, 6)
    for dim, parts in pieces:
        heights = jnp.exp(jax.random.uniform(jax.random.fold_in(own, dim), (parts,), jnp.float32, smallest / len(pieces), top_value / len(pieces)))
        loudness = loudness * jnp.repeat(heights, extent[dim] // parts).reshape([-1 if axis == dim else 1 for axis in range(len(extent))])
    return loudness


def gaussian(rng, shape, width, reach, split=(), kind=jnp.bfloat16):
    entries = width * jax.random.normal(rng, shape, jnp.float32)
    if split:
        entries = entries * block_scale(rng, shape, split, -0.22, 0.18)
    return jnp.clip(entries, -reach, reach).astype(kind)


def setup_inputs(seed: int = 0) -> dict:
    seeds = jax.random.split(jax.random.key(seed), 9)
    trial_states = gaussian(seeds[0], (TRIALS, 2, NPW), 1.0, 6.0, ((0, 8), (2, 32)), jnp.float32)
    resident = gaussian(seeds[1], (RES, 2, NPW), 1.0, 6.0, ((0, 8), (2, 32)))
    potential = jnp.clip(-1.0 + 3.0 * jax.random.uniform(seeds[2], (NG, NG, NG), jnp.float32) ** block_scale(seeds[2], (NG, NG, NG), ((0, 32),), -0.2, 0.2), -1.0, 2.0)
    stick_columns = draw_stick_columns(jax.random.fold_in(seeds[8], 71), 0)
    gvector_cells = draw_gvector_cells(jax.random.fold_in(seeds[8], 71), 0)
    slab_owner = jax.random.permutation(seeds[5], N_ROW).astype(jnp.int32)
    panel_owner = draw_panel_owner(jax.random.fold_in(seeds[8], 71), 0)
    rotation = gaussian(seeds[7], (PANELS * RES_DEV, RES), (PANELS * RES_DEV) ** -0.5, 0.5, ((1, 8),))
    return {"trial_states": trial_states, "resident": resident, "potential": potential, "stick_columns": stick_columns, "gvector_cells": gvector_cells, "slab_owner": slab_owner, "panel_owner": panel_owner, "rotation": rotation}


def frequency(grid_index):
    return jnp.where(grid_index < NG // 2, grid_index, grid_index - NG).astype(jnp.float32)


def reference(trial_states, resident, potential, stick_columns, gvector_cells, slab_owner, panel_owner, rotation):
    row_of = jnp.arange(NPW, dtype=jnp.int32) // NPW_DEV
    z_cell = gvector_cells // STK_DEV
    stick_index = row_of * STK_DEV + gvector_cells % STK_DEV
    column = stick_columns[stick_index]
    x_cell = column // NG
    y_cell = column % NG
    kinetic = 2.0 * (frequency(x_cell) ** 2 + frequency(y_cell) ** 2 + frequency(z_cell) ** 2) / (NG * NG)
    blocks = potential.reshape(N_ROW, NZD, NG, NG)
    full_potential = jnp.zeros((N_ROW, NZD, NG, NG), jnp.float32).at[slab_owner].set(blocks).reshape(NG, NG, NG)

    def apply_one(coefficient):
        zero_grid = jnp.zeros((NG, NG, NG), jnp.float32)
        grid_values = lax.complex(zero_grid.at[z_cell, x_cell, y_cell].set(coefficient[0]),
                                  zero_grid.at[z_cell, x_cell, y_cell].set(coefficient[1]))
        real_space = jnp.fft.ifftn(grid_values, norm="ortho")
        returned = jnp.fft.fftn(full_potential * real_space, norm="ortho")
        picked = returned[z_cell, x_cell, y_cell]
        return jnp.stack([jnp.real(picked) + kinetic * coefficient[0], jnp.imag(picked) + kinetic * coefficient[1]])

    applied = lax.map(apply_one, trial_states)
    resident_rows = resident.reshape(RES, 2 * NPW)
    accumulated = jnp.zeros((RES, 2 * NPW), jnp.float32)
    for panel_index in range(PANELS):
        panel_block = lax.dynamic_slice_in_dim(resident_rows, (panel_owner[panel_index] * RES_DEV).astype(jnp.int32), RES_DEV, 0)
        weights = rotation[panel_index * RES_DEV:(panel_index + 1) * RES_DEV]
        accumulated = accumulated + jnp.dot(weights.T, panel_block, preferred_element_type=jnp.float32)
    rotated = accumulated.astype(jnp.bfloat16).reshape(RES, 2, NPW)
    return (applied, rotated)
```

```python
import jax
import jax.numpy as jnp
import numpy as np
from jax import lax
from jax.experimental import pallas as pl
from jax.experimental.pallas import tpu as pltpu
from jax.sharding import PartitionSpec as P

NG = 128
ROWS = 32
XS = 4
CH = 4
GR = 4
MESH = pl.DeviceIdType.MESH
F32 = jnp.float32
BF = jnp.bfloat16
NT = (((1,), (1,)), ((), ()))


def dot(a, b):
    return jnp.dot(a, b, preferred_element_type=F32)


def dot_nt(a, b):
    return lax.dot_general(a, b, NT, preferred_element_type=F32)


def onehot(key, size):
    rows = lax.broadcasted_iota(jnp.int32, (size, key.shape[-1]), 0)
    return jnp.where(rows == key, 1.0, 0.0).astype(BF)


def frequency(j):
    return jnp.where(j < NG // 2, j, j - NG).astype(F32)


def tables():
    phase = 2.0 * np.pi / NG * (np.outer(np.arange(NG), np.arange(NG)) % NG)
    c, s = np.cos(phase), np.sin(phase)
    base = np.block([[c, -s], [s, c]])
    return jnp.asarray(np.stack([base, base.T]), BF)


def kernel(
    trial, resident, potential, columns, cells, slab, owner, rotation, table,
    applied, rotated,
    all_columns, stick_hot, plane_hot, kinetic, sent1, got1, sent2, got2,
    grid, picked, panels, own_part, part_out, part_in, weight_out, weight_in,
    col_send, col_recv, s1, r1, s2, r2, xs, xr, zs, zr, ws, wr,
):
    col = lax.axis_index("col")
    row = lax.axis_index("row")
    half = col // XS
    x = lax.rem(col, XS)
    mate = lax.rem(col + XS, 2 * XS)
    npw = cells.shape[-1]
    width = npw // CH

    def x_peer(d):
        return half * XS + lax.rem(x + d, XS)

    barrier = pltpu.get_barrier_semaphore()

    def greet(d, carry):
        pl.semaphore_signal(
            barrier, inc=1, device_id=(col, lax.rem(row + d, ROWS)), device_id_type=MESH
        )
        return carry

    lax.fori_loop(1, ROWS, greet, 0)
    for d in range(1, XS):
        pl.semaphore_signal(barrier, inc=1, device_id=(x_peer(d), row), device_id_type=MESH)
    pl.semaphore_signal(barrier, inc=1, device_id=(mate, row), device_id_type=MESH)

    for c in range(CH):
        block = resident[:, :, c * width:(c + 1) * width].reshape(32, width)
        panels[c, pl.ds(x, 1)] = block[None]

    lane = lax.broadcasted_iota(jnp.int32, (16, NG), 1)
    sub = lax.broadcasted_iota(jnp.int32, (16, NG), 0)
    perm = jnp.concatenate(
        [jnp.where(lane == owner[p] * 16 + sub, 1.0, 0.0) for p in range(8)], axis=0
    ).astype(BF)
    by_group = dot(rotation[...], perm).astype(BF)
    up = jnp.where(
        lax.broadcasted_iota(jnp.int32, (32, 16), 0) // 2
        == lax.broadcasted_iota(jnp.int32, (32, 16), 1), 1.0, 0.0).astype(BF)
    out = jnp.where(
        lax.broadcasted_iota(jnp.int32, (NG, 256), 1) // 2
        == lax.broadcasted_iota(jnp.int32, (NG, 256), 0), 1.0, 0.0).astype(BF)
    spread = dot(dot(up, by_group).astype(BF), out)
    same = (
        lax.broadcasted_iota(jnp.int32, (32, 256), 0) % 2
        == lax.broadcasted_iota(jnp.int32, (32, 256), 1) % 2
    )
    spread = jnp.where(same, spread, 0.0)
    weight_own = jnp.where(half == 0, spread[:, :NG], spread[:, NG:]).astype(BF)
    weight_out[...] = jnp.where(half == 0, spread[:, NG:], spread[:, :NG]).astype(BF)
    all_columns[pl.ds(row, 1)] = columns[...].reshape(1, 1, NG)

    for c in range(8):
        cell = cells[:, c * 512:(c + 1) * 512]
        z = cell // NG
        stick_hot[:, c * 512:(c + 1) * 512] = onehot((z // 64) * NG + cell % NG, 256)

    pl.semaphore_wait(barrier, ROWS - 1 + XS - 1 + 1)

    def send_columns(d, carry):
        pltpu.make_async_remote_copy(
            columns, all_columns.at[row], col_send, col_recv,
            device_id=(col, lax.rem(row + d, ROWS)), device_id_type=MESH,
        ).start()
        return carry

    lax.fori_loop(1, ROWS, send_columns, 0)
    w_copy = pltpu.make_async_remote_copy(
        weight_out, weight_in, ws, wr, device_id=(mate, row), device_id_type=MESH
    )
    w_copy.start()

    def x_copy(c, d):
        return pltpu.make_async_remote_copy(
            panels.at[c, x], panels.at[c, x], xs.at[c, d - 1], xr.at[c, d - 1],
            device_id=(x_peer(d), row), device_id_type=MESH,
        )

    def x_arrival(c, d):
        return pltpu.make_async_remote_copy(
            panels.at[c, x], panels.at[c, lax.rem(x + XS - d, XS)], xs.at[c, d - 1], xr.at[c, d - 1],
            device_id=(x_peer(d), row), device_id_type=MESH,
        )

    for c in range(CH):
        for d in (2, 1, 3):
            x_copy(c, d).start()

    def stick_part(c, acc):
        at = pl.ds(pl.multiple_of(c * 512, 512), 512)
        zh = cells[:, at] // NG % 64
        hit = lax.broadcasted_iota(jnp.int32, (64, 512), 0) == zh
        left = jnp.concatenate(
            [jnp.where(hit, trial[s, p:p + 1, at], 0.0) for s in range(2) for p in range(2)],
            axis=0,
        ).astype(BF)
        return acc + dot_nt(left, stick_hot[:, at])

    filled = lax.fori_loop(0, 8, stick_part, jnp.zeros((256, 256), F32))
    filled = jnp.concatenate(
        [
            jnp.concatenate(
                [filled[(2 * s + p) * 64:(2 * s + p + 1) * 64, u * NG:(u + 1) * NG]
                 for p in range(2) for u in range(2)], axis=0)
            for s in range(2)
        ], axis=1).astype(BF)

    j = lax.broadcasted_iota(jnp.int32, (8, 256), 0)
    k = lax.broadcasted_iota(jnp.int32, (8, 256), 1)
    want = j // 4 * NG + j % 4
    order = jnp.concatenate(
        [jnp.where(k == want + slab[r] * 4, 1.0, 0.0) for r in range(ROWS)], axis=0
    ).astype(BF)
    depth_inverse = dot(order, table[0]).astype(BF)
    depth_forward = dot_nt(table[1], order).astype(BF)
    spread_z = dot(depth_inverse, filled)
    for r in range(ROWS):
        rows = slice(8 * r, 8 * r + 8)
        sent1[r] = jnp.concatenate([spread_z[rows, :NG], spread_z[rows, NG:]], axis=0).astype(BF)

    def exchange(source, target, send_sem, recv_sem):
        def go(d, carry):
            to = lax.rem(row + d, ROWS)
            pltpu.make_async_remote_copy(
                source.at[to], target.at[row], send_sem, recv_sem,
                device_id=(col, to), device_id_type=MESH,
            ).start()
            return carry

        lax.fori_loop(1, ROWS, go, 0)
        pltpu.make_async_copy(source.at[row], target.at[row], recv_sem).start()

    exchange(sent1, got1, s1, r1.at[row // (ROWS // GR)])

    own_col = columns[...]
    fx, fy = frequency(own_col // NG), frequency(own_col % NG)
    rows16 = lax.broadcasted_iota(jnp.int32, (16, NG), 0)
    fxy = jnp.where(rows16 == 0, fx, jnp.where(rows16 == 1, fy, 0.0))
    fxy = jnp.concatenate([fxy, fxy], axis=1).astype(BF)
    for c in range(8):
        at = slice(c * 512, (c + 1) * 512)
        f = dot(fxy, stick_hot[:, at])
        fz = frequency(cells[:, at] // NG)
        kinetic[:, at] = 2.0 * (f[0:1] * f[0:1] + f[1:2] * f[1:2] + fz * fz) / (NG * NG)

    pltpu.make_async_copy(all_columns.at[pl.ds(0, ROWS - 1)], all_columns.at[pl.ds(0, ROWS - 1)], col_recv).wait()
    for c in range(8):
        key = jnp.concatenate([all_columns[4 * c + i] for i in range(4)], axis=1)
        plane_hot[:, c * 512:(c + 1) * 512] = onehot(key // (64 * NG) * NG + key % NG, 256)

    def rotate(c):
        if c == 0:
            w_copy.wait()
        for d in range(1, XS):
            x_arrival(c, d).wait_recv()
        both = jnp.concatenate([weight_own, weight_in[...]], axis=0)
        r = dot(both, panels[c].reshape(4 * 32, width))
        own_part[c] = r[:32]
        part_out[c] = r[32:].astype(BF)
        z_copy(c).start()

    def z_copy(c):
        return pltpu.make_async_remote_copy(
            part_out.at[c], part_in.at[c], zs.at[c], zr.at[c],
            device_id=(mate, row), device_id_type=MESH,
        )

    per = ROWS // GR
    for g in range(GR):
        pltpu.make_async_copy(got1.at[pl.ds(g * per, per)], got1.at[pl.ds(g * per, per)], r1.at[g]).wait()
        key = jnp.concatenate([all_columns[per * g + i] for i in range(per)], axis=1)
        hit = lax.broadcasted_iota(jnp.int32, (64, per * NG), 0) == key // NG % 64
        values = jnp.concatenate([got1[per * g + i] for i in range(per)], axis=1).astype(F32)
        right = plane_hot[:, g * per * NG:(g + 1) * per * NG]
        for m in range(4):
            left = jnp.concatenate(
                [jnp.where(hit, values[4 * m + i:4 * m + i + 1], 0.0) for i in range(4)], axis=0
            ).astype(BF)
            part = dot_nt(left, right)
            if g == 0:
                grid[256 * m:256 * m + 256] = part
            else:
                grid[256 * m:256 * m + 256] += part

    rotate(0)
    forward_x, forward_y = table[0], table[1]
    for s in range(2):
        for q in range(4):
            cp = [(s * 2 + p) * 4 + q for p in range(2)]
            block = jnp.concatenate(
                [grid[i * 64:(i + 1) * 64, u * NG:(u + 1) * NG] for i in cp for u in range(2)],
                axis=0).astype(BF)
            t = dot(table[0], block)
            t = jnp.concatenate([t[:NG], t[NG:]], axis=1).astype(BF)
            t = dot(t, table[1])
            v = potential[q] * (2.0 ** -21)
            t = (t * jnp.concatenate([v, v], axis=1)).astype(BF)
            t = dot(t, table[0])
            t = jnp.concatenate([t[:, :NG], t[:, NG:]], axis=0).astype(BF)
            t = dot(table[1], t).astype(BF)
            for p in range(2):
                picked[cp[p] * 64:(cp[p] + 1) * 64] = jnp.concatenate(
                    [t[p * NG:p * NG + 64], t[p * NG + 64:p * NG + NG]], axis=1)

    rotate(1)

    def pick(n, carry):
        pair = lax.rem(row // 2 + n, ROWS // 2)
        at = pl.ds(pl.multiple_of(pair * 256, 256), 256)
        u = dot(picked[...], plane_hot[:, at])
        key = jnp.concatenate([all_columns[2 * pair], all_columns[2 * pair + 1]], axis=1)
        hit = lax.broadcasted_iota(jnp.int32, (64, 256), 0) == key // NG % 64
        got = jnp.concatenate(
            [jnp.sum(jnp.where(hit, u[i * 64:(i + 1) * 64], 0.0), axis=0, keepdims=True)
             for i in range(16)], axis=0).astype(BF)
        for i in range(2):
            to = 2 * pair + i
            sent2[to] = got[:, i * NG:(i + 1) * NG]

            @pl.when(to != row)
            def _():
                pltpu.make_async_remote_copy(
                    sent2.at[to], got2.at[row], s2, r2,
                    device_id=(col, to), device_id_type=MESH,
                ).start()

        return carry

    lax.fori_loop(0, ROWS // 2, pick, 0)
    pltpu.make_async_copy(sent2.at[row], got2.at[row], r2).start()
    rotate(2)
    rotate(3)

    pltpu.make_async_copy(got2, got2, r2).wait()
    back = got2[...].astype(F32).reshape(ROWS, 2, 8, NG)
    back = jnp.concatenate(
        [back[:, 0].reshape(256, NG), back[:, 1].reshape(256, NG)], axis=1).astype(BF)
    back = dot(depth_forward, back).astype(BF)
    back = jnp.concatenate(
        [
            jnp.concatenate(
                [back[p * NG + u * 64:p * NG + u * 64 + 64, s * NG:(s + 1) * NG] for u in range(2)],
                axis=1)
            for s in range(2) for p in range(2)
        ], axis=0)
    for c in range(8):
        at = slice(c * 512, (c + 1) * 512)
        u = dot(back, stick_hot[:, at])
        hit = lax.broadcasted_iota(jnp.int32, (64, 512), 0) == cells[:, at] // NG % 64
        kin = kinetic[:, at]
        for s in range(2):
            v = jnp.concatenate(
                [jnp.sum(jnp.where(hit, u[(2 * s + p) * 64:(2 * s + p + 1) * 64], 0.0),
                         axis=0, keepdims=True) for p in range(2)], axis=0)
            applied[s, :, at] = v + kin * trial[s, :, at]

    for c in range(CH):
        z_copy(c).wait_recv()
        total = own_part[c] + part_in[c].astype(F32)
        rotated[:, :, c * width:(c + 1) * width] = total.astype(BF).reshape(16, 2, width)

    pltpu.make_async_copy(all_columns.at[pl.ds(0, ROWS - 1)], all_columns.at[pl.ds(0, ROWS - 1)], col_send).wait()
    for sem in (s1, s2):
        pltpu.make_async_copy(got2.at[pl.ds(0, ROWS - 1)], got2.at[pl.ds(0, ROWS - 1)], sem).wait()
    for c in range(CH):
        for d in range(1, XS):
            x_copy(c, d).wait_send()
        z_copy(c).wait_send()


def local(trial, resident, potential, columns, cells, slab, owner, rotation):
    npw = cells.shape[0]
    width = npw // CH
    vmem = pl.BlockSpec(memory_space=pltpu.VMEM)
    smem = pl.BlockSpec(memory_space=pltpu.SMEM)
    dma = pltpu.SemaphoreType.DMA
    return pl.pallas_call(
        kernel,
        out_shape=(
            jax.ShapeDtypeStruct(trial.shape, F32),
            jax.ShapeDtypeStruct(resident.shape, BF),
        ),
        in_specs=[vmem, vmem, vmem, vmem, vmem, smem, smem, vmem, vmem],
        out_specs=(vmem, vmem),
        scratch_shapes=[
            pltpu.VMEM((ROWS, 1, NG), jnp.int32),
            pltpu.VMEM((256, npw), BF),
            pltpu.VMEM((256, ROWS * NG), BF),
            pltpu.VMEM((1, npw), F32),
            pltpu.VMEM((ROWS, 16, NG), BF),
            pltpu.VMEM((ROWS, 16, NG), BF),
            pltpu.VMEM((ROWS, 16, NG), BF),
            pltpu.VMEM((ROWS, 16, NG), BF),
            pltpu.VMEM((1024, 256), F32),
            pltpu.VMEM((1024, 256), BF),
            pltpu.VMEM((CH, XS, 32, width), BF),
            pltpu.VMEM((CH, 32, width), F32),
            pltpu.VMEM((CH, 32, width), BF),
            pltpu.VMEM((CH, 32, width), BF),
            pltpu.VMEM((32, NG), BF),
            pltpu.VMEM((32, NG), BF),
            dma, dma, dma, dma((GR,)), dma, dma,
            dma((CH, XS - 1)), dma((CH, XS - 1)), dma((CH,)), dma((CH,)), dma, dma,
        ],
        compiler_params=pltpu.CompilerParams(
            collective_id=0, has_side_effects=True, vmem_limit_bytes=48 * 2**20
        ),
        cost_estimate=pl.CostEstimate(
            flops=4 * 10**9, bytes_accessed=2 * 10**6, transcendentals=0
        ),
    )(
        trial, resident, potential, columns.reshape(1, NG), cells.reshape(1, npw),
        slab, owner, rotation.T, tables(),
    )


def solution(mesh):
    return jax.shard_map(
        local,
        mesh=mesh,
        in_specs=(
            P("col", None, "row"), P("col", None, "row"), P("row", None, None),
            P("row"), P("row"), P(), P(), P(None, "col"),
        ),
        out_specs=(P("col", None, "row"), P("col", None, "row")),
        check_vma=False,
    )
```

```python
import jax
import jax.numpy as jnp
import numpy as np
from jax import lax
from jax.experimental import pallas as pl
from jax.experimental.pallas import tpu as pltpu
from jax.sharding import PartitionSpec as P

NG = 128
ROWS = 32
XS = 4
PAIRS = ROWS // 2
CH = 8
EARLY = 4
PLAN = {"start": (0,), "fill1": (1,), "fill3": (2,), "plane0": (3,), "plane1": (4,), "pick7": (5,), "pick15": (6,), "end": (7,)}
GR = 4
MESH = pl.DeviceIdType.MESH
F32 = jnp.float32
BF = jnp.bfloat16
NT = (((1,), (1,)), ((), ()))


def dot(a, b):
    return jnp.dot(a, b, preferred_element_type=F32)


def dot_nt(a, b):
    return lax.dot_general(a, b, NT, preferred_element_type=F32)


def onehot(key, size):
    rows = lax.broadcasted_iota(jnp.int32, (size, key.shape[-1]), 0)
    return jnp.where(rows == key, 1.0, 0.0).astype(BF)


def frequency(j):
    return jnp.where(j < NG // 2, j, j - NG).astype(F32)


def make_table(table):
    a = lax.broadcasted_iota(jnp.int32, (NG, NG), 0)
    b = lax.broadcasted_iota(jnp.int32, (NG, NG), 1)
    step = lax.broadcasted_iota(jnp.int32, (8, NG), 1).astype(F32)
    wave = jnp.tile(jnp.cos(step * (2.0 * np.pi / NG)), (NG // 8, 1))
    k = a * b
    c = jnp.take_along_axis(wave, k % NG, axis=1)
    s = jnp.take_along_axis(wave, (k + 3 * NG // 4) % NG, axis=1)
    top = jnp.concatenate([c, -s], axis=1)
    flip = jnp.concatenate([c, s], axis=1)
    low = jnp.concatenate([s, c], axis=1)
    table[0] = jnp.concatenate([top, low], axis=0).astype(BF)
    low = jnp.concatenate([-s, c], axis=1)
    table[1] = jnp.concatenate([flip, low], axis=0).astype(BF)


def kernel(
    trial_in, resident_in, potential_in, columns_in, cells_in, slab_in, owner_in, rotation_in,
    applied, rotated,
    trial, resident, potential, columns, cells, slab, owner, rotation, table, loads,
    all_columns, stick_hot, plane_hot, kinetic, sent1, got1, sent2, got2,
    grid, picked, panels, own_part, part_out, part_in, weight_out, weight_in,
    col_send, col_recv, s1, r1, s2, r2, xs, xr, zs, zr, ws, wr,
):
    col = lax.axis_index("col")
    row = lax.axis_index("row")
    half = col // XS
    x = lax.rem(col, XS)
    mate = lax.rem(col + XS, 2 * XS)
    pair = row // 2
    core = lax.rem(row, 2)
    sibling = row + 1 - 2 * core
    npw = cells_in.shape[-1]
    width = npw // CH

    def x_peer(d):
        return half * XS + lax.rem(x + d, XS)

    def peer(q, i):
        return lax.rem(pair + q, PAIRS) * 2 + i

    def slot(q):
        return lax.rem(PAIRS - q, PAIRS) * 2 + core

    load = [
        pltpu.make_async_copy(source, target, loads.at[i])
        for i, (source, target) in enumerate((
            (columns_in, columns), (cells_in, cells), (resident_in, resident),
            (rotation_in, rotation), (trial_in, trial), (potential_in, potential),
            (slab_in, slab), (owner_in, owner),
        ))
    ]
    for i in (1, 4, 2, 0, 6, 3, 7, 5):
        load[i].start()

    barrier = pltpu.get_barrier_semaphore()

    def greet(d, carry):
        pl.semaphore_signal(
            barrier, inc=1, device_id=(col, lax.rem(row + d, ROWS)), device_id_type=MESH
        )
        return carry

    lax.fori_loop(1, ROWS, greet, 0)
    for d in range(1, XS):
        pl.semaphore_signal(barrier, inc=1, device_id=(x_peer(d), row), device_id_type=MESH)
    pl.semaphore_signal(barrier, inc=1, device_id=(mate, row), device_id_type=MESH)

    make_table(table)

    load[1].wait()
    load[4].wait()

    def stick_part(c):
        at = slice(c * 512, (c + 1) * 512)
        cell = cells[:, at]
        z = cell // NG
        hot = onehot((z // 64) * NG + cell % NG, 256)
        stick_hot[:, at] = hot
        hit = lax.broadcasted_iota(jnp.int32, (64, 512), 0) == z % 64
        left = jnp.concatenate(
            [jnp.where(hit, trial[s, p:p + 1, at], 0.0) for s in range(2) for p in range(2)],
            axis=0,
        ).astype(BF)
        return dot_nt(left, hot)

    def sticks(first, last, acc=None):
        for c in range(first, last):
            acc = stick_part(c) if acc is None else acc + stick_part(c)
        return acc

    filled = sticks(0, EARLY) if EARLY else None

    load[2].wait()
    for c in range(CH):
        block = resident[:, :, c * width:(c + 1) * width].reshape(32, width)
        panels[c, pl.ds(x, 1)] = block[None]
    load[0].wait()
    all_columns[pl.ds(core, 1)] = columns[...].reshape(1, 1, NG)

    pl.semaphore_wait(barrier, ROWS - 1 + XS - 1 + 1)

    def x_copy(c, d):
        return pltpu.make_async_remote_copy(
            panels.at[c, x], panels.at[c, x], xs.at[c, d - 1], xr.at[c, d - 1],
            device_id=(x_peer(d), row), device_id_type=MESH,
        )

    def x_arrival(c, d):
        return pltpu.make_async_remote_copy(
            panels.at[c, x], panels.at[c, lax.rem(x + XS - d, XS)], xs.at[c, d - 1], xr.at[c, d - 1],
            device_id=(x_peer(d), row), device_id_type=MESH,
        )

    def send_column(q, i, to):
        pltpu.make_async_remote_copy(
            columns, all_columns.at[slot(q)], col_send, col_recv,
            device_id=(col, to), device_id_type=MESH,
        ).start()

    for d in (2, 1, 3):
        x_copy(0, d).start()
    send_column(0, 0, sibling)

    def send_columns(q, carry):
        send_column(q, 0, peer(q, 0))
        send_column(q, 1, peer(q, 1))
        return carry

    lax.fori_loop(1, PAIRS, send_columns, 0)
    for c in range(1, CH):
        for d in (2, 1, 3):
            x_copy(c, d).start()

    filled = sticks(EARLY, 8, filled)
    filled = jnp.concatenate(
        [
            jnp.concatenate(
                [filled[(2 * s + p) * 64:(2 * s + p + 1) * 64, u * NG:(u + 1) * NG]
                 for p in range(2) for u in range(2)], axis=0)
            for s in range(2)
        ], axis=1).astype(BF)

    load[6].wait()
    j = lax.broadcasted_iota(jnp.int32, (8, 256), 0)
    k = lax.broadcasted_iota(jnp.int32, (8, 256), 1)
    want = j // 4 * NG + j % 4
    order = jnp.concatenate(
        [jnp.where(k == want + slab[r] * 4, 1.0, 0.0) for r in range(ROWS)], axis=0
    ).astype(BF)
    depth_inverse = dot(order, table[0]).astype(BF)
    spread_z = dot(depth_inverse, filled)
    for r in range(ROWS):
        rows = slice(8 * r, 8 * r + 8)
        sent1[r] = jnp.concatenate([spread_z[rows, :NG], spread_z[rows, NG:]], axis=0).astype(BF)

    def send_stick(q, to):
        at = slot(q)
        pltpu.make_async_remote_copy(
            sent1.at[to], got1.at[at], s1, r1.at[at // (ROWS // GR)],
            device_id=(col, to), device_id_type=MESH,
        ).start()

    send_stick(0, sibling)

    def send_sticks(n, carry):
        q = PAIRS - n
        send_stick(q, peer(q, 0))
        send_stick(q, peer(q, 1))
        return carry

    lax.fori_loop(1, PAIRS, send_sticks, 0)
    pltpu.make_async_copy(sent1.at[row], got1.at[core], r1.at[0]).start()

    load[3].wait()
    load[7].wait()
    lane = lax.broadcasted_iota(jnp.int32, (16, NG), 1)
    sub = lax.broadcasted_iota(jnp.int32, (16, NG), 0)
    perm = jnp.concatenate(
        [jnp.where(lane == owner[p] * 16 + sub, 1.0, 0.0) for p in range(8)], axis=0
    ).astype(BF)
    by_group = dot(rotation[...], perm).astype(BF)
    up = jnp.where(
        lax.broadcasted_iota(jnp.int32, (32, 16), 0) // 2
        == lax.broadcasted_iota(jnp.int32, (32, 16), 1), 1.0, 0.0).astype(BF)
    out = jnp.where(
        lax.broadcasted_iota(jnp.int32, (NG, 256), 1) // 2
        == lax.broadcasted_iota(jnp.int32, (NG, 256), 0), 1.0, 0.0).astype(BF)
    spread = dot(dot(up, by_group).astype(BF), out)
    same = (
        lax.broadcasted_iota(jnp.int32, (32, 256), 0) % 2
        == lax.broadcasted_iota(jnp.int32, (32, 256), 1) % 2
    )
    spread = jnp.where(same, spread, 0.0)
    weight_own = jnp.where(half == 0, spread[:, :NG], spread[:, NG:]).astype(BF)
    weight_out[...] = jnp.where(half == 0, spread[:, NG:], spread[:, :NG]).astype(BF)
    w_copy = pltpu.make_async_remote_copy(
        weight_out, weight_in, ws, wr, device_id=(mate, row), device_id_type=MESH
    )
    w_copy.start()

    pltpu.make_async_copy(all_columns.at[pl.ds(0, ROWS - 1)], all_columns.at[pl.ds(0, ROWS - 1)], col_recv).wait()
    for c in range(8):
        key = jnp.concatenate([all_columns[4 * c + i] for i in range(4)], axis=1)
        plane_hot[:, c * 512:(c + 1) * 512] = onehot(key // (64 * NG) * NG + key % NG, 256)

    def rotate(c):
        if c == 0:
            w_copy.wait()
        for d in range(1, XS):
            x_arrival(c, d).wait_recv()
        both = jnp.concatenate([weight_own, weight_in[...]], axis=0)
        r = dot(both, panels[c].reshape(4 * 32, width))
        own_part[c] = r[:32]
        part_out[c] = r[32:].astype(BF)
        z_copy(c).start()

    def z_copy(c):
        return pltpu.make_async_remote_copy(
            part_out.at[c], part_in.at[c], zs.at[c], zr.at[c],
            device_id=(mate, row), device_id_type=MESH,
        )

    def rotations(place):
        for c in PLAN.get(place, ()):
            rotate(c)

    rotations("start")

    per = ROWS // GR
    for g in range(GR):
        pltpu.make_async_copy(got1.at[pl.ds(g * per, per)], got1.at[pl.ds(g * per, per)], r1.at[g]).wait()
        key = jnp.concatenate([all_columns[per * g + i] for i in range(per)], axis=1)
        hit = lax.broadcasted_iota(jnp.int32, (64, per * NG), 0) == key // NG % 64
        values = jnp.concatenate([got1[per * g + i] for i in range(per)], axis=1).astype(F32)
        right = plane_hot[:, g * per * NG:(g + 1) * per * NG]
        for m in range(4):
            left = jnp.concatenate(
                [jnp.where(hit, values[4 * m + i:4 * m + i + 1], 0.0) for i in range(4)], axis=0
            ).astype(BF)
            part = dot_nt(left, right)
            if g == 0:
                grid[256 * m:256 * m + 256] = part
            else:
                grid[256 * m:256 * m + 256] += part
        rotations("fill%d" % g)

    load[5].wait()
    for s in range(2):
        for q in range(4):
            cp = [(s * 2 + p) * 4 + q for p in range(2)]
            block = jnp.concatenate(
                [grid[i * 64:(i + 1) * 64, u * NG:(u + 1) * NG] for i in cp for u in range(2)],
                axis=0).astype(BF)
            t = dot(table[0], block)
            t = jnp.concatenate([t[:NG], t[NG:]], axis=1).astype(BF)
            t = dot(t, table[1])
            v = potential[q] * (2.0 ** -21)
            t = (t * jnp.concatenate([v, v], axis=1)).astype(BF)
            t = dot(t, table[0])
            t = jnp.concatenate([t[:, :NG], t[:, NG:]], axis=0).astype(BF)
            t = dot(table[1], t).astype(BF)
            for p in range(2):
                picked[cp[p] * 64:(cp[p] + 1) * 64] = jnp.concatenate(
                    [t[p * NG:p * NG + 64], t[p * NG + 64:p * NG + NG]], axis=1)
        rotations("plane%d" % s)

    for q in range(PAIRS):
        u = dot(picked[...], plane_hot[:, q * 256:q * 256 + 256])
        key = jnp.concatenate([all_columns[2 * q], all_columns[2 * q + 1]], axis=1)
        hit = lax.broadcasted_iota(jnp.int32, (64, 256), 0) == key // NG % 64
        got = jnp.concatenate(
            [jnp.sum(jnp.where(hit, u[i * 64:(i + 1) * 64], 0.0), axis=0, keepdims=True)
             for i in range(16)], axis=0).astype(BF)
        for i in range(2):
            sent2[2 * q + i] = got[:, i * NG:(i + 1) * NG]
        for i in range(2) if q else (0,):
            pltpu.make_async_remote_copy(
                sent2.at[2 * q + i] if q else sent2.at[1 - core], got2.at[row], s2, r2,
                device_id=(col, peer(q, i) if q else sibling), device_id_type=MESH,
            ).start()
        rotations("pick%d" % q)
    pltpu.make_async_copy(sent2.at[core], got2.at[row], r2).start()

    own_col = columns[...]
    fx, fy = frequency(own_col // NG), frequency(own_col % NG)
    rows16 = lax.broadcasted_iota(jnp.int32, (16, NG), 0)
    fxy = jnp.where(rows16 == 0, fx, jnp.where(rows16 == 1, fy, 0.0))
    fxy = jnp.concatenate([fxy, fxy], axis=1).astype(BF)
    for c in range(8):
        at = slice(c * 512, (c + 1) * 512)
        f = dot(fxy, stick_hot[:, at])
        fz = frequency(cells[:, at] // NG)
        kinetic[:, at] = 2.0 * (f[0:1] * f[0:1] + f[1:2] * f[1:2] + fz * fz) / (NG * NG)
    depth_forward = dot_nt(table[1], order).astype(BF)
    rotations("end")

    pltpu.make_async_copy(got2, got2, r2).wait()
    back = got2[...].astype(F32).reshape(ROWS, 2, 8, NG)
    back = jnp.concatenate(
        [back[:, 0].reshape(256, NG), back[:, 1].reshape(256, NG)], axis=1).astype(BF)
    back = dot(depth_forward, back).astype(BF)
    back = jnp.concatenate(
        [
            jnp.concatenate(
                [back[p * NG + u * 64:p * NG + u * 64 + 64, s * NG:(s + 1) * NG] for u in range(2)],
                axis=1)
            for s in range(2) for p in range(2)
        ], axis=0)
    for c in range(8):
        at = slice(c * 512, (c + 1) * 512)
        u = dot(back, stick_hot[:, at])
        hit = lax.broadcasted_iota(jnp.int32, (64, 512), 0) == cells[:, at] // NG % 64
        kin = kinetic[:, at]
        for s in range(2):
            v = jnp.concatenate(
                [jnp.sum(jnp.where(hit, u[(2 * s + p) * 64:(2 * s + p + 1) * 64], 0.0),
                         axis=0, keepdims=True) for p in range(2)], axis=0)
            applied[s, :, at] = v + kin * trial[s, :, at]

    for c in range(CH):
        z_copy(c).wait_recv()
        total = own_part[c] + part_in[c].astype(F32)
        rotated[:, :, c * width:(c + 1) * width] = total.astype(BF).reshape(16, 2, width)

    pltpu.make_async_copy(all_columns.at[pl.ds(0, ROWS - 1)], all_columns.at[pl.ds(0, ROWS - 1)], col_send).wait()
    for sem in (s1, s2):
        pltpu.make_async_copy(got2.at[pl.ds(0, ROWS - 1)], got2.at[pl.ds(0, ROWS - 1)], sem).wait()
    for c in range(CH):
        for d in range(1, XS):
            x_copy(c, d).wait_send()
        z_copy(c).wait_send()


def local(trial, resident, potential, columns, cells, slab, owner, rotation):
    npw = cells.shape[0]
    width = npw // CH
    vmem = pl.BlockSpec(memory_space=pltpu.VMEM)
    hbm = pl.BlockSpec(memory_space=pl.ANY)
    dma = pltpu.SemaphoreType.DMA
    return pl.pallas_call(
        kernel,
        out_shape=(
            pltpu.VMEM(trial.shape, F32),
            pltpu.VMEM(resident.shape, BF),
        ),
        in_specs=[hbm] * 8,
        out_specs=(vmem, vmem),
        scratch_shapes=[
            pltpu.VMEM(trial.shape, F32),
            pltpu.VMEM(resident.shape, BF),
            pltpu.VMEM(potential.shape, F32),
            pltpu.VMEM((1, NG), jnp.int32),
            pltpu.VMEM((1, npw), jnp.int32),
            pltpu.SMEM((ROWS,), jnp.int32),
            pltpu.SMEM((8,), jnp.int32),
            pltpu.VMEM((16, NG), BF),
            pltpu.VMEM((2, 256, 256), BF),
            dma((8,)),
            pltpu.VMEM((ROWS, 1, NG), jnp.int32),
            pltpu.VMEM((256, npw), BF),
            pltpu.VMEM((256, ROWS * NG), BF),
            pltpu.VMEM((1, npw), F32),
            pltpu.VMEM((ROWS, 16, NG), BF),
            pltpu.VMEM((ROWS, 16, NG), BF),
            pltpu.VMEM((ROWS, 16, NG), BF),
            pltpu.VMEM((ROWS, 16, NG), BF),
            pltpu.VMEM((1024, 256), F32),
            pltpu.VMEM((1024, 256), BF),
            pltpu.VMEM((CH, XS, 32, width), BF),
            pltpu.VMEM((CH, 32, width), F32),
            pltpu.VMEM((CH, 32, width), BF),
            pltpu.VMEM((CH, 32, width), BF),
            pltpu.VMEM((32, NG), BF),
            pltpu.VMEM((32, NG), BF),
            dma, dma, dma, dma((GR,)), dma, dma,
            dma((CH, XS - 1)), dma((CH, XS - 1)), dma((CH,)), dma((CH,)), dma, dma,
        ],
        compiler_params=pltpu.CompilerParams(
            collective_id=0, has_side_effects=True, vmem_limit_bytes=48 * 2**20
        ),
        cost_estimate=pl.CostEstimate(
            flops=4 * 10**9, bytes_accessed=2 * 10**6, transcendentals=0
        ),
    )(*(
        pltpu.with_memory_space_constraint(operand, pltpu.HBM)
        for operand in (
            trial, resident, potential, columns.reshape(1, NG), cells.reshape(1, npw),
            slab, owner, rotation.T,
        )
    ))


def solution(mesh):
    return jax.shard_map(
        local,
        mesh=mesh,
        in_specs=(
            P("col", None, "row"), P("col", None, "row"), P("row", None, None),
            P("row"), P("row"), P(), P(), P(None, "col"),
        ),
        out_specs=(P("col", None, "row"), P("col", None, "row")),
        check_vma=False,
    )
```

```python
import jax
import jax.numpy as jnp
import numpy as np
from jax import lax
from jax.experimental import pallas as pl
from jax.experimental.pallas import tpu as pltpu
from jax.sharding import PartitionSpec as P

NG = 128
ROWS = 32
XS = 4
PAIRS = ROWS // 2
CH = 8
EARLY = 0
LATE = 2
PLAN = {"sent": (0,), "start": (1,), "fill1": (2,), "fill3": (3,), "plane0": (4,), "plane1": (5,), "pick5": (6,), "pick10": (7,)}
GR = 4
MESH = pl.DeviceIdType.MESH
F32 = jnp.float32
BF = jnp.bfloat16
NT = (((1,), (1,)), ((), ()))


def dot(a, b):
    return jnp.dot(a, b, preferred_element_type=F32)


def dot_nt(a, b):
    return lax.dot_general(a, b, NT, preferred_element_type=F32)


def onehot(key, size):
    rows = lax.broadcasted_iota(jnp.int32, (size, key.shape[-1]), 0)
    return jnp.where(rows == key, 1.0, 0.0).astype(BF)


def frequency(j):
    return jnp.where(j < NG // 2, j, j - NG).astype(F32)


def make_table(table):
    a = lax.broadcasted_iota(jnp.int32, (NG, NG), 0)
    b = lax.broadcasted_iota(jnp.int32, (NG, NG), 1)
    step = lax.broadcasted_iota(jnp.int32, (8, NG), 1).astype(F32)
    wave = jnp.tile(jnp.cos(step * (2.0 * np.pi / NG)), (NG // 8, 1))
    k = a * b
    c = jnp.take_along_axis(wave, k % NG, axis=1)
    s = jnp.take_along_axis(wave, (k + 3 * NG // 4) % NG, axis=1)
    top = jnp.concatenate([c, -s], axis=1)
    flip = jnp.concatenate([c, s], axis=1)
    low = jnp.concatenate([s, c], axis=1)
    table[0] = jnp.concatenate([top, low], axis=0).astype(BF)
    low = jnp.concatenate([-s, c], axis=1)
    table[1] = jnp.concatenate([flip, low], axis=0).astype(BF)


def kernel(
    trial_in, resident_in, potential_in, columns_in, cells_in, slab_in, owner_in, rotation_in,
    applied, rotated,
    trial, resident, potential, columns, cells, slab, owner, rotation, table, loads,
    all_columns, stick_hot, plane_hot, kinetic, sent1, got1, sent2, got2,
    grid, picked, panels, own_part, part_out, part_in, weight_out, weight_in,
    col_send, col_recv, s1, r1, s2, r2, xs, xr, zs, zr, ws, wr,
):
    col = lax.axis_index("col")
    row = lax.axis_index("row")
    half = col // XS
    x = lax.rem(col, XS)
    mate = lax.rem(col + XS, 2 * XS)
    pair = row // 2
    core = lax.rem(row, 2)
    sibling = row + 1 - 2 * core
    npw = cells_in.shape[-1]
    width = npw // CH

    def x_peer(d):
        return half * XS + lax.rem(x + d, XS)

    def peer(q, i):
        return lax.rem(pair + q, PAIRS) * 2 + i

    def slot(q):
        return lax.rem(PAIRS - q, PAIRS) * 2 + core

    load = [
        pltpu.make_async_copy(source, target, loads.at[i])
        for i, (source, target) in enumerate((
            (columns_in, columns), (cells_in, cells), (resident_in, resident),
            (rotation_in, rotation), (trial_in, trial), (potential_in, potential),
            (slab_in, slab), (owner_in, owner),
        ))
    ]
    for i in (1, 4, 2, 0, 6, 3, 7, 5):
        load[i].start()

    barrier = pltpu.get_barrier_semaphore()

    def greet(d, carry):
        pl.semaphore_signal(
            barrier, inc=1, device_id=(col, lax.rem(row + d, ROWS)), device_id_type=MESH
        )
        return carry

    lax.fori_loop(1, ROWS, greet, 0)
    for d in range(1, XS):
        pl.semaphore_signal(barrier, inc=1, device_id=(x_peer(d), row), device_id_type=MESH)
    pl.semaphore_signal(barrier, inc=1, device_id=(mate, row), device_id_type=MESH)

    make_table(table)

    load[1].wait()
    load[4].wait()

    def stick_part(c):
        at = slice(c * 512, (c + 1) * 512)
        cell = cells[:, at]
        z = cell // NG
        hot = onehot((z // 64) * NG + cell % NG, 256)
        stick_hot[:, at] = hot
        hit = lax.broadcasted_iota(jnp.int32, (64, 512), 0) == z % 64
        left = jnp.concatenate(
            [jnp.where(hit, trial[s, p:p + 1, at], 0.0) for s in range(2) for p in range(2)],
            axis=0,
        ).astype(BF)
        return dot_nt(left, hot)

    def sticks(first, last, acc=None):
        for c in range(first, last):
            acc = stick_part(c) if acc is None else acc + stick_part(c)
        return acc

    filled = sticks(0, EARLY) if EARLY else None

    load[2].wait()
    for c in range(CH):
        block = resident[:, :, c * width:(c + 1) * width].reshape(32, width)
        panels[c, pl.ds(x, 1)] = block[None]
    load[0].wait()
    all_columns[pl.ds(core, 1)] = columns[...].reshape(1, 1, NG)

    load[3].wait()
    load[7].wait()
    lane = lax.broadcasted_iota(jnp.int32, (16, NG), 1)
    sub = lax.broadcasted_iota(jnp.int32, (16, NG), 0)
    perm = jnp.concatenate(
        [jnp.where(lane == owner[p] * 16 + sub, 1.0, 0.0) for p in range(8)], axis=0
    ).astype(BF)
    by_group = dot(rotation[...], perm).astype(BF)
    up = jnp.where(
        lax.broadcasted_iota(jnp.int32, (32, 16), 0) // 2
        == lax.broadcasted_iota(jnp.int32, (32, 16), 1), 1.0, 0.0).astype(BF)
    out = jnp.where(
        lax.broadcasted_iota(jnp.int32, (NG, 256), 1) // 2
        == lax.broadcasted_iota(jnp.int32, (NG, 256), 0), 1.0, 0.0).astype(BF)
    spread = dot(dot(up, by_group).astype(BF), out)
    same = (
        lax.broadcasted_iota(jnp.int32, (32, 256), 0) % 2
        == lax.broadcasted_iota(jnp.int32, (32, 256), 1) % 2
    )
    spread = jnp.where(same, spread, 0.0)
    weight_own = jnp.where(half == 0, spread[:, :NG], spread[:, NG:]).astype(BF)
    weight_out[...] = jnp.where(half == 0, spread[:, NG:], spread[:, :NG]).astype(BF)
    pl.semaphore_wait(barrier, ROWS - 1 + XS - 1 + 1)

    w_copy = pltpu.make_async_remote_copy(
        weight_out, weight_in, ws, wr, device_id=(mate, row), device_id_type=MESH
    )
    w_copy.start()

    def x_copy(c, d):
        return pltpu.make_async_remote_copy(
            panels.at[c, x], panels.at[c, x], xs.at[c, d - 1], xr.at[c, d - 1],
            device_id=(x_peer(d), row), device_id_type=MESH,
        )

    def x_arrival(c, d):
        return pltpu.make_async_remote_copy(
            panels.at[c, x], panels.at[c, lax.rem(x + XS - d, XS)], xs.at[c, d - 1], xr.at[c, d - 1],
            device_id=(x_peer(d), row), device_id_type=MESH,
        )

    def rotate(c):
        if c == 0:
            w_copy.wait()
        for d in range(1, XS):
            x_arrival(c, d).wait_recv()
        both = jnp.concatenate([weight_own, weight_in[...]], axis=0)
        r = dot(both, panels[c].reshape(4 * 32, width))
        own_part[c] = r[:32]
        part_out[c] = r[32:].astype(BF)
        z_copy(c).start()

    def z_copy(c):
        return pltpu.make_async_remote_copy(
            part_out.at[c], part_in.at[c], zs.at[c], zr.at[c],
            device_id=(mate, row), device_id_type=MESH,
        )

    def rotations(place):
        for c in PLAN.get(place, ()):
            rotate(c)

    def send_column(q, i, to):
        pltpu.make_async_remote_copy(
            columns, all_columns.at[slot(q)], col_send, col_recv,
            device_id=(col, to), device_id_type=MESH,
        ).start()

    for d in (2, 1, 3):
        x_copy(0, d).start()
    send_column(0, 0, sibling)

    def send_columns(q, carry):
        send_column(q, 0, peer(q, 0))
        send_column(q, 1, peer(q, 1))
        return carry

    lax.fori_loop(1, PAIRS, send_columns, 0)
    for c in range(1, LATE):
        for d in (2, 1, 3):
            x_copy(c, d).start()

    filled = sticks(EARLY, 8, filled)
    filled = jnp.concatenate(
        [
            jnp.concatenate(
                [filled[(2 * s + p) * 64:(2 * s + p + 1) * 64, u * NG:(u + 1) * NG]
                 for p in range(2) for u in range(2)], axis=0)
            for s in range(2)
        ], axis=1).astype(BF)

    load[6].wait()
    j = lax.broadcasted_iota(jnp.int32, (8, 256), 0)
    k = lax.broadcasted_iota(jnp.int32, (8, 256), 1)
    want = j // 4 * NG + j % 4
    order = jnp.concatenate(
        [jnp.where(k == want + slab[r] * 4, 1.0, 0.0) for r in range(ROWS)], axis=0
    ).astype(BF)
    depth_inverse = dot(order, table[0]).astype(BF)
    spread_z = dot(depth_inverse, filled)
    for r in range(ROWS):
        rows = slice(8 * r, 8 * r + 8)
        sent1[r] = jnp.concatenate([spread_z[rows, :NG], spread_z[rows, NG:]], axis=0).astype(BF)

    def send_stick(q, to):
        at = slot(q)
        pltpu.make_async_remote_copy(
            sent1.at[to], got1.at[at], s1, r1.at[at // (ROWS // GR)],
            device_id=(col, to), device_id_type=MESH,
        ).start()

    send_stick(0, sibling)

    def send_sticks(n, carry):
        q = PAIRS - n
        send_stick(q, peer(q, 0))
        send_stick(q, peer(q, 1))
        return carry

    lax.fori_loop(1, PAIRS, send_sticks, 0)
    pltpu.make_async_copy(sent1.at[row], got1.at[core], r1.at[0]).start()
    for c in range(LATE, CH):
        for d in (2, 1, 3):
            x_copy(c, d).start()
    rotations("sent")


    pltpu.make_async_copy(all_columns.at[pl.ds(0, ROWS - 1)], all_columns.at[pl.ds(0, ROWS - 1)], col_recv).wait()
    for c in range(8):
        key = jnp.concatenate([all_columns[4 * c + i] for i in range(4)], axis=1)
        plane_hot[:, c * 512:(c + 1) * 512] = onehot(key // (64 * NG) * NG + key % NG, 256)

    rotations("start")

    per = ROWS // GR
    for g in range(GR):
        pltpu.make_async_copy(got1.at[pl.ds(g * per, per)], got1.at[pl.ds(g * per, per)], r1.at[g]).wait()
        key = jnp.concatenate([all_columns[per * g + i] for i in range(per)], axis=1)
        hit = lax.broadcasted_iota(jnp.int32, (64, per * NG), 0) == key // NG % 64
        values = jnp.concatenate([got1[per * g + i] for i in range(per)], axis=1).astype(F32)
        right = plane_hot[:, g * per * NG:(g + 1) * per * NG]
        for m in range(4):
            left = jnp.concatenate(
                [jnp.where(hit, values[4 * m + i:4 * m + i + 1], 0.0) for i in range(4)], axis=0
            ).astype(BF)
            part = dot_nt(left, right)
            if g == 0:
                grid[256 * m:256 * m + 256] = part
            else:
                grid[256 * m:256 * m + 256] += part
        rotations("fill%d" % g)

    load[5].wait()
    level = jnp.concatenate([potential[q] for q in range(4)], axis=0) * (2.0 ** -21)
    level = jnp.concatenate([level, level], axis=1)
    for s in range(2):
        t = jnp.concatenate(
            [
                jnp.concatenate(
                    [grid[i * 64:(i + 1) * 64, u * NG:(u + 1) * NG]
                     for i in (8 * s + q, 8 * s + 4 + q) for u in range(2)], axis=0)
                for q in range(4)
            ], axis=1).astype(BF)
        t = dot(table[0], t).astype(BF)
        t = jnp.concatenate(
            [jnp.concatenate([t[:NG, q * NG:(q + 1) * NG], t[NG:, q * NG:(q + 1) * NG]], axis=1)
             for q in range(4)], axis=0)
        t = dot(t, table[1])
        t = (t * level).astype(BF)
        t = dot(t, table[0]).astype(BF)
        t = jnp.concatenate(
            [jnp.concatenate([t[q * NG:(q + 1) * NG, :NG], t[q * NG:(q + 1) * NG, NG:]], axis=0)
             for q in range(4)], axis=1)
        t = dot(table[1], t).astype(BF)
        for q in range(4):
            for p in range(2):
                picked[((2 * s + p) * 4 + q) * 64:((2 * s + p) * 4 + q + 1) * 64] = jnp.concatenate(
                    [t[p * NG + u * 64:p * NG + u * 64 + 64, q * NG:(q + 1) * NG] for u in range(2)],
                    axis=1)
        rotations("plane%d" % s)

    for q in range(PAIRS):
        u = dot(picked[...], plane_hot[:, q * 256:q * 256 + 256])
        key = jnp.concatenate([all_columns[2 * q], all_columns[2 * q + 1]], axis=1)
        hit = lax.broadcasted_iota(jnp.int32, (64, 256), 0) == key // NG % 64
        got = jnp.concatenate(
            [jnp.sum(jnp.where(hit, u[i * 64:(i + 1) * 64], 0.0), axis=0, keepdims=True)
             for i in range(16)], axis=0).astype(BF)
        for i in range(2):
            sent2[2 * q + i] = got[:, i * NG:(i + 1) * NG]
        for i in range(2) if q else (0,):
            pltpu.make_async_remote_copy(
                sent2.at[2 * q + i] if q else sent2.at[1 - core], got2.at[row], s2, r2,
                device_id=(col, peer(q, i) if q else sibling), device_id_type=MESH,
            ).start()
        rotations("pick%d" % q)
    pltpu.make_async_copy(sent2.at[core], got2.at[row], r2).start()

    own_col = columns[...]
    fx, fy = frequency(own_col // NG), frequency(own_col % NG)
    rows16 = lax.broadcasted_iota(jnp.int32, (16, NG), 0)
    fxy = jnp.where(rows16 == 0, fx, jnp.where(rows16 == 1, fy, 0.0))
    fxy = jnp.concatenate([fxy, fxy], axis=1).astype(BF)
    for c in range(8):
        at = slice(c * 512, (c + 1) * 512)
        f = dot(fxy, stick_hot[:, at])
        fz = frequency(cells[:, at] // NG)
        kinetic[:, at] = 2.0 * (f[0:1] * f[0:1] + f[1:2] * f[1:2] + fz * fz) / (NG * NG)
    depth_forward = dot_nt(table[1], order).astype(BF)
    rotations("end")

    pltpu.make_async_copy(got2, got2, r2).wait()
    back = got2[...].astype(F32).reshape(ROWS, 2, 8, NG)
    back = jnp.concatenate(
        [back[:, 0].reshape(256, NG), back[:, 1].reshape(256, NG)], axis=1).astype(BF)
    back = dot(depth_forward, back).astype(BF)
    back = jnp.concatenate(
        [
            jnp.concatenate(
                [back[p * NG + u * 64:p * NG + u * 64 + 64, s * NG:(s + 1) * NG] for u in range(2)],
                axis=1)
            for s in range(2) for p in range(2)
        ], axis=0)
    for c in range(8):
        at = slice(c * 512, (c + 1) * 512)
        u = dot(back, stick_hot[:, at])
        hit = lax.broadcasted_iota(jnp.int32, (64, 512), 0) == cells[:, at] // NG % 64
        kin = kinetic[:, at]
        for s in range(2):
            v = jnp.concatenate(
                [jnp.sum(jnp.where(hit, u[(2 * s + p) * 64:(2 * s + p + 1) * 64], 0.0),
                         axis=0, keepdims=True) for p in range(2)], axis=0)
            applied[s, :, at] = v + kin * trial[s, :, at]

    for c in range(CH):
        z_copy(c).wait_recv()
        total = own_part[c] + part_in[c].astype(F32)
        rotated[:, :, c * width:(c + 1) * width] = total.astype(BF).reshape(16, 2, width)

    pltpu.make_async_copy(all_columns.at[pl.ds(0, ROWS - 1)], all_columns.at[pl.ds(0, ROWS - 1)], col_send).wait()
    for sem in (s1, s2):
        pltpu.make_async_copy(got2.at[pl.ds(0, ROWS - 1)], got2.at[pl.ds(0, ROWS - 1)], sem).wait()
    for c in range(CH):
        for d in range(1, XS):
            x_copy(c, d).wait_send()
        z_copy(c).wait_send()


def local(trial, resident, potential, columns, cells, slab, owner, rotation):
    npw = cells.shape[0]
    width = npw // CH
    vmem = pl.BlockSpec(memory_space=pltpu.VMEM)
    hbm = pl.BlockSpec(memory_space=pl.ANY)
    dma = pltpu.SemaphoreType.DMA
    return pl.pallas_call(
        kernel,
        out_shape=(
            pltpu.VMEM(trial.shape, F32),
            pltpu.VMEM(resident.shape, BF),
        ),
        in_specs=[hbm] * 8,
        out_specs=(vmem, vmem),
        scratch_shapes=[
            pltpu.VMEM(trial.shape, F32),
            pltpu.VMEM(resident.shape, BF),
            pltpu.VMEM(potential.shape, F32),
            pltpu.VMEM((1, NG), jnp.int32),
            pltpu.VMEM((1, npw), jnp.int32),
            pltpu.SMEM((ROWS,), jnp.int32),
            pltpu.SMEM((8,), jnp.int32),
            pltpu.VMEM((16, NG), BF),
            pltpu.VMEM((2, 256, 256), BF),
            dma((8,)),
            pltpu.VMEM((ROWS, 1, NG), jnp.int32),
            pltpu.VMEM((256, npw), BF),
            pltpu.VMEM((256, ROWS * NG), BF),
            pltpu.VMEM((1, npw), F32),
            pltpu.VMEM((ROWS, 16, NG), BF),
            pltpu.VMEM((ROWS, 16, NG), BF),
            pltpu.VMEM((ROWS, 16, NG), BF),
            pltpu.VMEM((ROWS, 16, NG), BF),
            pltpu.VMEM((1024, 256), F32),
            pltpu.VMEM((1024, 256), BF),
            pltpu.VMEM((CH, XS, 32, width), BF),
            pltpu.VMEM((CH, 32, width), F32),
            pltpu.VMEM((CH, 32, width), BF),
            pltpu.VMEM((CH, 32, width), BF),
            pltpu.VMEM((32, NG), BF),
            pltpu.VMEM((32, NG), BF),
            dma, dma, dma, dma((GR,)), dma, dma,
            dma((CH, XS - 1)), dma((CH, XS - 1)), dma((CH,)), dma((CH,)), dma, dma,
        ],
        compiler_params=pltpu.CompilerParams(
            collective_id=0, has_side_effects=True, vmem_limit_bytes=48 * 2**20
        ),
        cost_estimate=pl.CostEstimate(
            flops=4 * 10**9, bytes_accessed=2 * 10**6, transcendentals=0
        ),
    )(*(
        pltpu.with_memory_space_constraint(operand, pltpu.HBM)
        for operand in (
            trial, resident, potential, columns.reshape(1, NG), cells.reshape(1, npw),
            slab, owner, rotation.T,
        )
    ))


def solution(mesh):
    return jax.shard_map(
        local,
        mesh=mesh,
        in_specs=(
            P("col", None, "row"), P("col", None, "row"), P("row", None, None),
            P("row"), P("row"), P(), P(), P(None, "col"),
        ),
        out_specs=(P("col", None, "row"), P("col", None, "row")),
        check_vma=False,
    )
```

```python
import jax
import jax.numpy as jnp
import numpy as np
from jax import lax
from jax.experimental import pallas as pl
from jax.experimental.pallas import tpu as pltpu
from jax.sharding import PartitionSpec as P

NG = 128
ROWS = 32
XS = 4
PAIRS = ROWS // 2
CH = 8
EARLY = 0
LATE = 2
RAW = 2
CUT = CH - RAW
PLAN = {"sent": (0,), "start": (1,), "fill0": (2,), "fill2": (3,), "fill3": (4,), "plane0": (5,), "end": (6, 7)}
PASS = {"start": (6,), "fill1": (7,)}
GR = 4
MESH = pl.DeviceIdType.MESH
F32 = jnp.float32
BF = jnp.bfloat16
NT = (((1,), (1,)), ((), ()))


def dot(a, b):
    return jnp.dot(a, b, preferred_element_type=F32)


def dot_nt(a, b):
    return lax.dot_general(a, b, NT, preferred_element_type=F32)


def onehot(key, size):
    rows = lax.broadcasted_iota(jnp.int32, (size, key.shape[-1]), 0)
    return jnp.where(rows == key, 1.0, 0.0).astype(BF)


def frequency(j):
    return jnp.where(j < NG // 2, j, j - NG).astype(F32)


def make_table(table):
    a = lax.broadcasted_iota(jnp.int32, (NG, NG), 0)
    b = lax.broadcasted_iota(jnp.int32, (NG, NG), 1)
    step = lax.broadcasted_iota(jnp.int32, (8, NG), 1).astype(F32)
    wave = jnp.tile(jnp.cos(step * (2.0 * np.pi / NG)), (NG // 8, 1))
    k = a * b
    c = jnp.take_along_axis(wave, k % NG, axis=1)
    s = jnp.take_along_axis(wave, (k + 3 * NG // 4) % NG, axis=1)
    top = jnp.concatenate([c, -s], axis=1)
    flip = jnp.concatenate([c, s], axis=1)
    low = jnp.concatenate([s, c], axis=1)
    table[0] = jnp.concatenate([top, low], axis=0).astype(BF)
    low = jnp.concatenate([-s, c], axis=1)
    table[1] = jnp.concatenate([flip, low], axis=0).astype(BF)


def kernel(
    trial_in, resident_in, potential_in, columns_in, cells_in, slab_in, owner_in, rotation_in,
    applied, rotated,
    trial, resident, potential, columns, cells, slab, owner, rotation, table, loads,
    all_columns, stick_hot, plane_hot, kinetic, sent1, got1, sent2, got2,
    grid, picked, panels, others, own_part, part_out, part_in, weight_out, weight_in,
    col_send, col_recv, s1, r1, s2, r2, xs, xr, zs, zr, ws, wr, fs, fr,
):
    col = lax.axis_index("col")
    row = lax.axis_index("row")
    half = col // XS
    x = lax.rem(col, XS)
    mate = lax.rem(col + XS, 2 * XS)
    pair = row // 2
    core = lax.rem(row, 2)
    sibling = row + 1 - 2 * core
    npw = cells_in.shape[-1]
    width = npw // CH

    def x_peer(d):
        return half * XS + lax.rem(x + d, XS)

    def peer(q, i):
        return lax.rem(pair + q, PAIRS) * 2 + i

    def slot(q):
        return lax.rem(PAIRS - q, PAIRS) * 2 + core

    load = [
        pltpu.make_async_copy(source, target, loads.at[i])
        for i, (source, target) in enumerate((
            (columns_in, columns), (cells_in, cells), (resident_in, resident),
            (rotation_in, rotation), (trial_in, trial), (potential_in, potential),
            (slab_in, slab), (owner_in, owner),
        ))
    ]
    for i in (1, 4, 2, 0, 6, 3, 7, 5):
        load[i].start()

    barrier = pltpu.get_barrier_semaphore()

    def greet(d, carry):
        pl.semaphore_signal(
            barrier, inc=1, device_id=(col, lax.rem(row + d, ROWS)), device_id_type=MESH
        )
        return carry

    lax.fori_loop(1, ROWS, greet, 0)
    for d in range(1, XS):
        pl.semaphore_signal(barrier, inc=1, device_id=(x_peer(d), row), device_id_type=MESH)
    pl.semaphore_signal(barrier, inc=1, device_id=(mate, row), device_id_type=MESH)

    make_table(table)

    load[1].wait()
    load[4].wait()

    def stick_part(c):
        at = slice(c * 512, (c + 1) * 512)
        cell = cells[:, at]
        z = cell // NG
        hot = onehot((z // 64) * NG + cell % NG, 256)
        stick_hot[:, at] = hot
        hit = lax.broadcasted_iota(jnp.int32, (64, 512), 0) == z % 64
        left = jnp.concatenate(
            [jnp.where(hit, trial[s, p:p + 1, at], 0.0) for s in range(2) for p in range(2)],
            axis=0,
        ).astype(BF)
        return dot_nt(left, hot)

    def sticks(first, last, acc=None):
        for c in range(first, last):
            acc = stick_part(c) if acc is None else acc + stick_part(c)
        return acc

    filled = sticks(0, EARLY) if EARLY else None

    load[2].wait()
    for c in range(CH):
        block = resident[:, :, c * width:(c + 1) * width].reshape(32, width)
        panels[c, pl.ds(x, 1)] = block[None]
    load[0].wait()
    all_columns[pl.ds(core, 1)] = columns[...].reshape(1, 1, NG)

    load[3].wait()
    load[7].wait()
    lane = lax.broadcasted_iota(jnp.int32, (16, NG), 1)
    sub = lax.broadcasted_iota(jnp.int32, (16, NG), 0)
    perm = jnp.concatenate(
        [jnp.where(lane == owner[p] * 16 + sub, 1.0, 0.0) for p in range(8)], axis=0
    ).astype(BF)
    by_group = dot(rotation[...], perm).astype(BF)
    up = jnp.where(
        lax.broadcasted_iota(jnp.int32, (32, 16), 0) // 2
        == lax.broadcasted_iota(jnp.int32, (32, 16), 1), 1.0, 0.0).astype(BF)
    out = jnp.where(
        lax.broadcasted_iota(jnp.int32, (NG, 256), 1) // 2
        == lax.broadcasted_iota(jnp.int32, (NG, 256), 0), 1.0, 0.0).astype(BF)
    spread = dot(dot(up, by_group).astype(BF), out)
    same = (
        lax.broadcasted_iota(jnp.int32, (32, 256), 0) % 2
        == lax.broadcasted_iota(jnp.int32, (32, 256), 1) % 2
    )
    spread = jnp.where(same, spread, 0.0)
    weight_own = jnp.where(half == 0, spread[:, :NG], spread[:, NG:]).astype(BF)
    weight_out[...] = jnp.where(half == 0, spread[:, NG:], spread[:, :NG]).astype(BF)
    pl.semaphore_wait(barrier, ROWS - 1 + XS - 1 + 1)

    w_copy = pltpu.make_async_remote_copy(
        weight_out, weight_in, ws, wr, device_id=(mate, row), device_id_type=MESH
    )
    w_copy.start()

    def x_copy(c, d):
        return pltpu.make_async_remote_copy(
            panels.at[c, x], panels.at[c, x], xs.at[c, d - 1], xr.at[c, d - 1],
            device_id=(x_peer(d), row), device_id_type=MESH,
        )

    def x_arrival(c, d):
        return pltpu.make_async_remote_copy(
            panels.at[c, x], panels.at[c, lax.rem(x + XS - d, XS)], xs.at[c, d - 1], xr.at[c, d - 1],
            device_id=(x_peer(d), row), device_id_type=MESH,
        )

    def rotate(c):
        if c == 0:
            w_copy.wait()
        for d in range(1, XS):
            x_arrival(c, d).wait_recv()
        both = jnp.concatenate([weight_own, weight_in[...]], axis=0)
        r = dot(both, panels[c].reshape(4 * 32, width))
        own_part[c] = r[:32]
        part_out[c] = r[32:].astype(BF)
        z_copy(c).start()

    def raw_copy(c):
        return pltpu.make_async_remote_copy(
            panels.at[c, x], others.at[c - CUT, x], zs.at[c], zr.at[c],
            device_id=(mate, row), device_id_type=MESH,
        )

    def pass_copy(c, d, at):
        return pltpu.make_async_remote_copy(
            others.at[c - CUT, x], others.at[c - CUT, at], fs.at[c - CUT, d - 1], fr.at[c - CUT, d - 1],
            device_id=(x_peer(d), row), device_id_type=MESH,
        )

    def pass_on(c):
        raw_copy(c).wait_recv()
        for d in (2, 1, 3):
            pass_copy(c, d, x).start()

    def rotate_raw(c):
        for d in range(1, XS):
            x_arrival(c, d).wait_recv()
            pass_copy(c, d, lax.rem(x + XS - d, XS)).wait_recv()
        r = dot(weight_own, panels[c].reshape(4 * 32, width))
        r = r + dot(weight_out[...], others[c - CUT].reshape(4 * 32, width))
        rotated[:, :, c * width:(c + 1) * width] = r.astype(BF).reshape(16, 2, width)

    def z_copy(c):
        return pltpu.make_async_remote_copy(
            part_out.at[c], part_in.at[c], zs.at[c], zr.at[c],
            device_id=(mate, row), device_id_type=MESH,
        )

    def rotations(place):
        for c in PASS.get(place, ()):
            pass_on(c)
        for c in PLAN.get(place, ()):
            (rotate if c < CUT else rotate_raw)(c)

    def send_column(q, i, to):
        pltpu.make_async_remote_copy(
            columns, all_columns.at[slot(q)], col_send, col_recv,
            device_id=(col, to), device_id_type=MESH,
        ).start()

    for c in range(CUT, CH):
        raw_copy(c).start()
    for d in (2, 1, 3):
        x_copy(0, d).start()
    send_column(0, 0, sibling)

    def send_columns(q, carry):
        send_column(q, 0, peer(q, 0))
        send_column(q, 1, peer(q, 1))
        return carry

    lax.fori_loop(1, PAIRS, send_columns, 0)
    for c in range(1, LATE):
        for d in (2, 1, 3):
            x_copy(c, d).start()

    filled = sticks(EARLY, 8, filled)
    filled = jnp.concatenate(
        [
            jnp.concatenate(
                [filled[(2 * s + p) * 64:(2 * s + p + 1) * 64, u * NG:(u + 1) * NG]
                 for p in range(2) for u in range(2)], axis=0)
            for s in range(2)
        ], axis=1).astype(BF)

    load[6].wait()
    j = lax.broadcasted_iota(jnp.int32, (8, 256), 0)
    k = lax.broadcasted_iota(jnp.int32, (8, 256), 1)
    want = j // 4 * NG + j % 4
    order = jnp.concatenate(
        [jnp.where(k == want + slab[r] * 4, 1.0, 0.0) for r in range(ROWS)], axis=0
    ).astype(BF)
    depth_inverse = dot(order, table[0]).astype(BF)
    spread_z = dot(depth_inverse, filled)
    for r in range(ROWS):
        rows = slice(8 * r, 8 * r + 8)
        sent1[r] = jnp.concatenate([spread_z[rows, :NG], spread_z[rows, NG:]], axis=0).astype(BF)

    def send_stick(q, to):
        at = slot(q)
        pltpu.make_async_remote_copy(
            sent1.at[to], got1.at[at], s1, r1.at[at // (ROWS // GR)],
            device_id=(col, to), device_id_type=MESH,
        ).start()

    send_stick(0, sibling)

    def send_sticks(n, carry):
        q = PAIRS - n
        send_stick(q, peer(q, 0))
        send_stick(q, peer(q, 1))
        return carry

    lax.fori_loop(1, PAIRS, send_sticks, 0)
    pltpu.make_async_copy(sent1.at[row], got1.at[core], r1.at[0]).start()
    for c in range(LATE, CH):
        for d in (2, 1, 3):
            x_copy(c, d).start()
    rotations("sent")


    pltpu.make_async_copy(all_columns.at[pl.ds(0, ROWS - 1)], all_columns.at[pl.ds(0, ROWS - 1)], col_recv).wait()
    for c in range(8):
        key = jnp.concatenate([all_columns[4 * c + i] for i in range(4)], axis=1)
        plane_hot[:, c * 512:(c + 1) * 512] = onehot(key // (64 * NG) * NG + key % NG, 256)

    rotations("start")

    per = ROWS // GR
    for g in range(GR):
        pltpu.make_async_copy(got1.at[pl.ds(g * per, per)], got1.at[pl.ds(g * per, per)], r1.at[g]).wait()
        key = jnp.concatenate([all_columns[per * g + i] for i in range(per)], axis=1)
        hit = lax.broadcasted_iota(jnp.int32, (64, per * NG), 0) == key // NG % 64
        values = jnp.concatenate([got1[per * g + i] for i in range(per)], axis=1).astype(F32)
        right = plane_hot[:, g * per * NG:(g + 1) * per * NG]
        for m in range(4):
            left = jnp.concatenate(
                [jnp.where(hit, values[4 * m + i:4 * m + i + 1], 0.0) for i in range(4)], axis=0
            ).astype(BF)
            part = dot_nt(left, right)
            if g == 0:
                grid[256 * m:256 * m + 256] = part
            else:
                grid[256 * m:256 * m + 256] += part
        rotations("fill%d" % g)

    load[5].wait()
    level = jnp.concatenate([potential[q] for q in range(4)], axis=0) * (2.0 ** -21)
    level = jnp.concatenate([level, level], axis=1)
    for s in range(2):
        t = jnp.concatenate(
            [
                jnp.concatenate(
                    [grid[i * 64:(i + 1) * 64, u * NG:(u + 1) * NG]
                     for i in (8 * s + q, 8 * s + 4 + q) for u in range(2)], axis=0)
                for q in range(4)
            ], axis=1).astype(BF)
        t = dot(table[0], t).astype(BF)
        t = jnp.concatenate(
            [jnp.concatenate([t[:NG, q * NG:(q + 1) * NG], t[NG:, q * NG:(q + 1) * NG]], axis=1)
             for q in range(4)], axis=0)
        t = dot(t, table[1])
        t = (t * level).astype(BF)
        t = dot(t, table[0]).astype(BF)
        t = jnp.concatenate(
            [jnp.concatenate([t[q * NG:(q + 1) * NG, :NG], t[q * NG:(q + 1) * NG, NG:]], axis=0)
             for q in range(4)], axis=1)
        t = dot(table[1], t).astype(BF)
        for q in range(4):
            for p in range(2):
                picked[((2 * s + p) * 4 + q) * 64:((2 * s + p) * 4 + q + 1) * 64] = jnp.concatenate(
                    [t[p * NG + u * 64:p * NG + u * 64 + 64, q * NG:(q + 1) * NG] for u in range(2)],
                    axis=1)
        rotations("plane%d" % s)

    for q in range(PAIRS):
        u = dot(picked[...], plane_hot[:, q * 256:q * 256 + 256])
        key = jnp.concatenate([all_columns[2 * q], all_columns[2 * q + 1]], axis=1)
        hit = lax.broadcasted_iota(jnp.int32, (64, 256), 0) == key // NG % 64
        got = jnp.concatenate(
            [jnp.sum(jnp.where(hit, u[i * 64:(i + 1) * 64], 0.0), axis=0, keepdims=True)
             for i in range(16)], axis=0).astype(BF)
        for i in range(2):
            sent2[2 * q + i] = got[:, i * NG:(i + 1) * NG]
        for i in range(2) if q else (0,):
            pltpu.make_async_remote_copy(
                sent2.at[2 * q + i] if q else sent2.at[1 - core], got2.at[row], s2, r2,
                device_id=(col, peer(q, i) if q else sibling), device_id_type=MESH,
            ).start()
        rotations("pick%d" % q)
    pltpu.make_async_copy(sent2.at[core], got2.at[row], r2).start()

    own_col = columns[...]
    fx, fy = frequency(own_col // NG), frequency(own_col % NG)
    rows16 = lax.broadcasted_iota(jnp.int32, (16, NG), 0)
    fxy = jnp.where(rows16 == 0, fx, jnp.where(rows16 == 1, fy, 0.0))
    fxy = jnp.concatenate([fxy, fxy], axis=1).astype(BF)
    for c in range(8):
        at = slice(c * 512, (c + 1) * 512)
        f = dot(fxy, stick_hot[:, at])
        fz = frequency(cells[:, at] // NG)
        kinetic[:, at] = 2.0 * (f[0:1] * f[0:1] + f[1:2] * f[1:2] + fz * fz) / (NG * NG)
    depth_forward = dot_nt(table[1], order).astype(BF)
    rotations("end")

    pltpu.make_async_copy(got2, got2, r2).wait()
    back = got2[...].astype(F32).reshape(ROWS, 2, 8, NG)
    back = jnp.concatenate(
        [back[:, 0].reshape(256, NG), back[:, 1].reshape(256, NG)], axis=1).astype(BF)
    back = dot(depth_forward, back).astype(BF)
    back = jnp.concatenate(
        [
            jnp.concatenate(
                [back[p * NG + u * 64:p * NG + u * 64 + 64, s * NG:(s + 1) * NG] for u in range(2)],
                axis=1)
            for s in range(2) for p in range(2)
        ], axis=0)
    for c in range(8):
        at = slice(c * 512, (c + 1) * 512)
        u = dot(back, stick_hot[:, at])
        hit = lax.broadcasted_iota(jnp.int32, (64, 512), 0) == cells[:, at] // NG % 64
        kin = kinetic[:, at]
        for s in range(2):
            v = jnp.concatenate(
                [jnp.sum(jnp.where(hit, u[(2 * s + p) * 64:(2 * s + p + 1) * 64], 0.0),
                         axis=0, keepdims=True) for p in range(2)], axis=0)
            applied[s, :, at] = v + kin * trial[s, :, at]
    rotations("last")

    for c in range(CUT):
        z_copy(c).wait_recv()
        total = own_part[c] + part_in[c].astype(F32)
        rotated[:, :, c * width:(c + 1) * width] = total.astype(BF).reshape(16, 2, width)

    pltpu.make_async_copy(all_columns.at[pl.ds(0, ROWS - 1)], all_columns.at[pl.ds(0, ROWS - 1)], col_send).wait()
    for sem in (s1, s2):
        pltpu.make_async_copy(got2.at[pl.ds(0, ROWS - 1)], got2.at[pl.ds(0, ROWS - 1)], sem).wait()
    for c in range(CH):
        for d in range(1, XS):
            x_copy(c, d).wait_send()
            if c >= CUT:
                pass_copy(c, d, x).wait_send()
        (z_copy if c < CUT else raw_copy)(c).wait_send()


def local(trial, resident, potential, columns, cells, slab, owner, rotation):
    npw = cells.shape[0]
    width = npw // CH
    vmem = pl.BlockSpec(memory_space=pltpu.VMEM)
    hbm = pl.BlockSpec(memory_space=pl.ANY)
    dma = pltpu.SemaphoreType.DMA
    return pl.pallas_call(
        kernel,
        out_shape=(
            pltpu.VMEM(trial.shape, F32),
            pltpu.VMEM(resident.shape, BF),
        ),
        in_specs=[hbm] * 8,
        out_specs=(vmem, vmem),
        scratch_shapes=[
            pltpu.VMEM(trial.shape, F32),
            pltpu.VMEM(resident.shape, BF),
            pltpu.VMEM(potential.shape, F32),
            pltpu.VMEM((1, NG), jnp.int32),
            pltpu.VMEM((1, npw), jnp.int32),
            pltpu.SMEM((ROWS,), jnp.int32),
            pltpu.SMEM((8,), jnp.int32),
            pltpu.VMEM((16, NG), BF),
            pltpu.VMEM((2, 256, 256), BF),
            dma((8,)),
            pltpu.VMEM((ROWS, 1, NG), jnp.int32),
            pltpu.VMEM((256, npw), BF),
            pltpu.VMEM((256, ROWS * NG), BF),
            pltpu.VMEM((1, npw), F32),
            pltpu.VMEM((ROWS, 16, NG), BF),
            pltpu.VMEM((ROWS, 16, NG), BF),
            pltpu.VMEM((ROWS, 16, NG), BF),
            pltpu.VMEM((ROWS, 16, NG), BF),
            pltpu.VMEM((1024, 256), F32),
            pltpu.VMEM((1024, 256), BF),
            pltpu.VMEM((CH, XS, 32, width), BF),
            pltpu.VMEM((RAW, XS, 32, width), BF),
            pltpu.VMEM((CH, 32, width), F32),
            pltpu.VMEM((CH, 32, width), BF),
            pltpu.VMEM((CH, 32, width), BF),
            pltpu.VMEM((32, NG), BF),
            pltpu.VMEM((32, NG), BF),
            dma, dma, dma, dma((GR,)), dma, dma,
            dma((CH, XS - 1)), dma((CH, XS - 1)), dma((CH,)), dma((CH,)), dma, dma,
            dma((RAW, XS - 1)), dma((RAW, XS - 1)),
        ],
        compiler_params=pltpu.CompilerParams(
            collective_id=0, has_side_effects=True, vmem_limit_bytes=48 * 2**20
        ),
        cost_estimate=pl.CostEstimate(
            flops=4 * 10**9, bytes_accessed=2 * 10**6, transcendentals=0
        ),
    )(*(
        pltpu.with_memory_space_constraint(operand, pltpu.HBM)
        for operand in (
            trial, resident, potential, columns.reshape(1, NG), cells.reshape(1, npw),
            slab, owner, rotation.T,
        )
    ))


def solution(mesh):
    return jax.shard_map(
        local,
        mesh=mesh,
        in_specs=(
            P("col", None, "row"), P("col", None, "row"), P("row", None, None),
            P("row"), P("row"), P(), P(), P(None, "col"),
        ),
        out_specs=(P("col", None, "row"), P("col", None, "row")),
        check_vma=False,
    )
```

```python
import jax
import jax.numpy as jnp
import numpy as np
from jax import lax
from jax.experimental import pallas as pl
from jax.experimental.pallas import tpu as pltpu
from jax.sharding import PartitionSpec as P

NG = 128
ROWS = 32
XS = 4
PAIRS = ROWS // 2
CH = 8
EARLY = 0
LATE = 2
RAW = 2
CUT = CH - RAW
PLAN = {"start": (0, 1), "fill0": (2,), "fill1": (3,), "fill2": (4,), "fill3": (5,), "end": (6, 7)}
PASS = {"fill1": (6,), "fill3": (7,)}
GR = 4
MESH = pl.DeviceIdType.MESH
F32 = jnp.float32
BF = jnp.bfloat16
NT = (((1,), (1,)), ((), ()))


def dot(a, b):
    return jnp.dot(a, b, preferred_element_type=F32)


def dot_nt(a, b):
    return lax.dot_general(a, b, NT, preferred_element_type=F32)


def onehot(key, size):
    rows = lax.broadcasted_iota(jnp.int32, (size, key.shape[-1]), 0)
    return jnp.where(rows == key, 1.0, 0.0).astype(BF)


def frequency(j):
    return jnp.where(j < NG // 2, j, j - NG).astype(F32)


def make_table(table):
    a = lax.broadcasted_iota(jnp.int32, (NG, NG), 0)
    b = lax.broadcasted_iota(jnp.int32, (NG, NG), 1)
    step = lax.broadcasted_iota(jnp.int32, (8, NG), 1).astype(F32)
    wave = jnp.tile(jnp.cos(step * (2.0 * np.pi / NG)), (NG // 8, 1))
    k = a * b
    c = jnp.take_along_axis(wave, k % NG, axis=1)
    s = jnp.take_along_axis(wave, (k + 3 * NG // 4) % NG, axis=1)
    top = jnp.concatenate([c, -s], axis=1)
    flip = jnp.concatenate([c, s], axis=1)
    low = jnp.concatenate([s, c], axis=1)
    table[0] = jnp.concatenate([top, low], axis=0).astype(BF)
    low = jnp.concatenate([-s, c], axis=1)
    table[1] = jnp.concatenate([flip, low], axis=0).astype(BF)


def kernel(
    trial_in, resident_in, potential_in, columns_in, cells_in, slab_in, owner_in, rotation_in,
    applied, rotated,
    trial, resident, potential, columns, cells, slab, owner, rotation, table, loads,
    all_columns, stick_hot, plane_hot, kinetic, sent1, got1, sent2, got2,
    grid, picked, panels, others, own_part, part_out, part_in, weight_out, weight_in,
    col_send, col_recv, s1, r1, s2, r2, xs, xr, zs, zr, ws, wr, fs, fr,
):
    col = lax.axis_index("col")
    row = lax.axis_index("row")
    half = col // XS
    x = lax.rem(col, XS)
    mate = lax.rem(col + XS, 2 * XS)
    pair = row // 2
    core = lax.rem(row, 2)
    sibling = row + 1 - 2 * core
    npw = cells_in.shape[-1]
    width = npw // CH

    def x_peer(d):
        return half * XS + lax.rem(x + d, XS)

    def peer(q, i):
        return lax.rem(pair + q, PAIRS) * 2 + i

    def slot(q):
        return lax.rem(PAIRS - q, PAIRS) * 2 + core

    load = [
        pltpu.make_async_copy(source, target, loads.at[i])
        for i, (source, target) in enumerate((
            (columns_in, columns), (cells_in, cells), (resident_in, resident),
            (rotation_in, rotation), (trial_in, trial), (potential_in, potential),
            (slab_in, slab), (owner_in, owner),
        ))
    ]
    for i in (1, 4, 2, 0, 6, 3, 7, 5):
        load[i].start()

    barrier = pltpu.get_barrier_semaphore()

    def greet(d, carry):
        pl.semaphore_signal(
            barrier, inc=1, device_id=(col, lax.rem(row + d, ROWS)), device_id_type=MESH
        )
        return carry

    lax.fori_loop(1, ROWS, greet, 0)
    for d in range(1, XS):
        pl.semaphore_signal(barrier, inc=1, device_id=(x_peer(d), row), device_id_type=MESH)
    pl.semaphore_signal(barrier, inc=1, device_id=(mate, row), device_id_type=MESH)

    make_table(table)

    load[1].wait()
    load[4].wait()

    def stick_part(c):
        at = slice(c * 512, (c + 1) * 512)
        cell = cells[:, at]
        z = cell // NG
        hot = onehot((z // 64) * NG + cell % NG, 256)
        stick_hot[:, at] = hot
        hit = lax.broadcasted_iota(jnp.int32, (64, 512), 0) == z % 64
        left = jnp.concatenate(
            [jnp.where(hit, trial[s, p:p + 1, at], 0.0) for s in range(2) for p in range(2)],
            axis=0,
        ).astype(BF)
        return dot_nt(left, hot)

    def sticks(first, last, acc=None):
        for c in range(first, last):
            acc = stick_part(c) if acc is None else acc + stick_part(c)
        return acc

    filled = sticks(0, EARLY) if EARLY else None

    load[2].wait()
    for c in range(CH):
        block = resident[:, :, c * width:(c + 1) * width].reshape(32, width)
        panels[c, pl.ds(x, 1)] = block[None]
    load[0].wait()
    all_columns[pl.ds(core, 1)] = columns[...].reshape(1, 1, NG)

    load[3].wait()
    load[7].wait()
    lane = lax.broadcasted_iota(jnp.int32, (16, NG), 1)
    sub = lax.broadcasted_iota(jnp.int32, (16, NG), 0)
    perm = jnp.concatenate(
        [jnp.where(lane == owner[p] * 16 + sub, 1.0, 0.0) for p in range(8)], axis=0
    ).astype(BF)
    by_group = dot(rotation[...], perm).astype(BF)
    up = jnp.where(
        lax.broadcasted_iota(jnp.int32, (32, 16), 0) // 2
        == lax.broadcasted_iota(jnp.int32, (32, 16), 1), 1.0, 0.0).astype(BF)
    out = jnp.where(
        lax.broadcasted_iota(jnp.int32, (NG, 256), 1) // 2
        == lax.broadcasted_iota(jnp.int32, (NG, 256), 0), 1.0, 0.0).astype(BF)
    spread = dot(dot(up, by_group).astype(BF), out)
    same = (
        lax.broadcasted_iota(jnp.int32, (32, 256), 0) % 2
        == lax.broadcasted_iota(jnp.int32, (32, 256), 1) % 2
    )
    spread = jnp.where(same, spread, 0.0)
    weight_own = jnp.where(half == 0, spread[:, :NG], spread[:, NG:]).astype(BF)
    weight_out[...] = jnp.where(half == 0, spread[:, NG:], spread[:, :NG]).astype(BF)
    pl.semaphore_wait(barrier, ROWS - 1 + XS - 1 + 1)

    w_copy = pltpu.make_async_remote_copy(
        weight_out, weight_in, ws, wr, device_id=(mate, row), device_id_type=MESH
    )
    w_copy.start()

    def x_copy(c, d):
        return pltpu.make_async_remote_copy(
            panels.at[c, x], panels.at[c, x], xs.at[c, d - 1], xr.at[c, d - 1],
            device_id=(x_peer(d), row), device_id_type=MESH,
        )

    def x_arrival(c, d):
        return pltpu.make_async_remote_copy(
            panels.at[c, x], panels.at[c, lax.rem(x + XS - d, XS)], xs.at[c, d - 1], xr.at[c, d - 1],
            device_id=(x_peer(d), row), device_id_type=MESH,
        )

    def rotate(c):
        if c == 0:
            w_copy.wait()
        for d in range(1, XS):
            x_arrival(c, d).wait_recv()
        both = jnp.concatenate([weight_own, weight_in[...]], axis=0)
        r = dot(both, panels[c].reshape(4 * 32, width))
        own_part[c] = r[:32]
        part_out[c] = r[32:].astype(BF)
        z_copy(c).start()

    def raw_copy(c):
        return pltpu.make_async_remote_copy(
            panels.at[c, x], others.at[c - CUT, x], zs.at[c], zr.at[c],
            device_id=(mate, row), device_id_type=MESH,
        )

    def pass_copy(c, d, at):
        return pltpu.make_async_remote_copy(
            others.at[c - CUT, x], others.at[c - CUT, at], fs.at[c - CUT, d - 1], fr.at[c - CUT, d - 1],
            device_id=(x_peer(d), row), device_id_type=MESH,
        )

    def pass_on(c):
        raw_copy(c).wait_recv()
        for d in (2, 1, 3):
            pass_copy(c, d, x).start()

    def rotate_raw(c):
        for d in range(1, XS):
            x_arrival(c, d).wait_recv()
            pass_copy(c, d, lax.rem(x + XS - d, XS)).wait_recv()
        r = dot(weight_own, panels[c].reshape(4 * 32, width))
        r = r + dot(weight_out[...], others[c - CUT].reshape(4 * 32, width))
        rotated[:, :, c * width:(c + 1) * width] = r.astype(BF).reshape(16, 2, width)

    def z_copy(c):
        return pltpu.make_async_remote_copy(
            part_out.at[c], part_in.at[c], zs.at[c], zr.at[c],
            device_id=(mate, row), device_id_type=MESH,
        )

    def rotations(place):
        for c in PASS.get(place, ()):
            pass_on(c)
        for c in PLAN.get(place, ()):
            (rotate if c < CUT else rotate_raw)(c)

    def send_column(q, i, to):
        pltpu.make_async_remote_copy(
            columns, all_columns.at[slot(q)], col_send, col_recv,
            device_id=(col, to), device_id_type=MESH,
        ).start()

    for c in range(CUT, CH):
        raw_copy(c).start()
    for d in (2, 1, 3):
        x_copy(0, d).start()
    send_column(0, 0, sibling)

    def send_columns(q, carry):
        send_column(q, 0, peer(q, 0))
        send_column(q, 1, peer(q, 1))
        return carry

    lax.fori_loop(1, PAIRS, send_columns, 0)
    for c in range(1, LATE):
        for d in (2, 1, 3):
            x_copy(c, d).start()

    filled = sticks(EARLY, 8, filled)
    filled = jnp.concatenate(
        [
            jnp.concatenate(
                [filled[(2 * s + p) * 64:(2 * s + p + 1) * 64, u * NG:(u + 1) * NG]
                 for p in range(2) for u in range(2)], axis=0)
            for s in range(2)
        ], axis=1).astype(BF)

    load[6].wait()
    j = lax.broadcasted_iota(jnp.int32, (8, 256), 0)
    k = lax.broadcasted_iota(jnp.int32, (8, 256), 1)
    want = j // 4 * NG + j % 4
    order = jnp.concatenate(
        [jnp.where(k == want + slab[r] * 4, 1.0, 0.0) for r in range(ROWS)], axis=0
    ).astype(BF)
    depth_inverse = dot(order, table[0]).astype(BF)
    spread_z = dot(depth_inverse, filled)
    for r in range(ROWS):
        rows = slice(8 * r, 8 * r + 8)
        sent1[r] = jnp.concatenate([spread_z[rows, :NG], spread_z[rows, NG:]], axis=0).astype(BF)

    def send_stick(q, to):
        at = slot(q)
        pltpu.make_async_remote_copy(
            sent1.at[to], got1.at[at], s1, r1.at[at // (ROWS // GR)],
            device_id=(col, to), device_id_type=MESH,
        ).start()

    send_stick(0, sibling)

    def send_sticks(n, carry):
        q = PAIRS - n
        send_stick(q, peer(q, 0))
        send_stick(q, peer(q, 1))
        return carry

    lax.fori_loop(1, PAIRS, send_sticks, 0)
    pltpu.make_async_copy(sent1.at[row], got1.at[core], r1.at[0]).start()
    for c in range(LATE, CH):
        for d in (2, 1, 3):
            x_copy(c, d).start()
    rotations("sent")


    pltpu.make_async_copy(all_columns.at[pl.ds(0, ROWS - 1)], all_columns.at[pl.ds(0, ROWS - 1)], col_recv).wait()
    for c in range(8):
        key = jnp.concatenate([all_columns[4 * c + i] for i in range(4)], axis=1)
        plane_hot[:, c * 512:(c + 1) * 512] = onehot(key // (64 * NG) * NG + key % NG, 256)

    rotations("start")

    per = ROWS // GR
    for g in range(GR):
        pltpu.make_async_copy(got1.at[pl.ds(g * per, per)], got1.at[pl.ds(g * per, per)], r1.at[g]).wait()
        key = jnp.concatenate([all_columns[per * g + i] for i in range(per)], axis=1)
        hit = lax.broadcasted_iota(jnp.int32, (64, per * NG), 0) == key // NG % 64
        values = jnp.concatenate([got1[per * g + i] for i in range(per)], axis=1).astype(F32)
        right = plane_hot[:, g * per * NG:(g + 1) * per * NG]
        for m in range(4):
            left = jnp.concatenate(
                [jnp.where(hit, values[4 * m + i:4 * m + i + 1], 0.0) for i in range(4)], axis=0
            ).astype(BF)
            part = dot_nt(left, right)
            if g == 0:
                grid[256 * m:256 * m + 256] = part
            else:
                grid[256 * m:256 * m + 256] += part
        rotations("fill%d" % g)

    load[5].wait()
    level = jnp.concatenate([potential[q] for q in range(4)], axis=0) * (2.0 ** -21)
    level = jnp.concatenate([level, level], axis=1)
    for s in range(2):
        t = jnp.concatenate(
            [
                jnp.concatenate(
                    [grid[i * 64:(i + 1) * 64, u * NG:(u + 1) * NG]
                     for i in (8 * s + q, 8 * s + 4 + q) for u in range(2)], axis=0)
                for q in range(4)
            ], axis=1).astype(BF)
        t = dot(table[0], t).astype(BF)
        t = jnp.concatenate(
            [jnp.concatenate([t[:NG, q * NG:(q + 1) * NG], t[NG:, q * NG:(q + 1) * NG]], axis=1)
             for q in range(4)], axis=0)
        t = dot(t, table[1])
        t = (t * level).astype(BF)
        t = dot(t, table[0]).astype(BF)
        t = jnp.concatenate(
            [jnp.concatenate([t[q * NG:(q + 1) * NG, :NG], t[q * NG:(q + 1) * NG, NG:]], axis=0)
             for q in range(4)], axis=1)
        t = dot(table[1], t).astype(BF)
        for q in range(4):
            for p in range(2):
                picked[((2 * s + p) * 4 + q) * 64:((2 * s + p) * 4 + q + 1) * 64] = jnp.concatenate(
                    [t[p * NG + u * 64:p * NG + u * 64 + 64, q * NG:(q + 1) * NG] for u in range(2)],
                    axis=1)
        rotations("plane%d" % s)

    for q in range(PAIRS):
        u = dot(picked[...], plane_hot[:, q * 256:q * 256 + 256])
        key = jnp.concatenate([all_columns[2 * q], all_columns[2 * q + 1]], axis=1)
        hit = lax.broadcasted_iota(jnp.int32, (64, 256), 0) == key // NG % 64
        got = jnp.concatenate(
            [jnp.sum(jnp.where(hit, u[i * 64:(i + 1) * 64], 0.0), axis=0, keepdims=True)
             for i in range(16)], axis=0).astype(BF)
        for i in range(2):
            sent2[2 * q + i] = got[:, i * NG:(i + 1) * NG]
        for i in range(2) if q else (0,):
            pltpu.make_async_remote_copy(
                sent2.at[2 * q + i] if q else sent2.at[1 - core], got2.at[row], s2, r2,
                device_id=(col, peer(q, i) if q else sibling), device_id_type=MESH,
            ).start()
        rotations("pick%d" % q)
    pltpu.make_async_copy(sent2.at[core], got2.at[row], r2).start()

    own_col = columns[...]
    fx, fy = frequency(own_col // NG), frequency(own_col % NG)
    rows16 = lax.broadcasted_iota(jnp.int32, (16, NG), 0)
    fxy = jnp.where(rows16 == 0, fx, jnp.where(rows16 == 1, fy, 0.0))
    fxy = jnp.concatenate([fxy, fxy], axis=1).astype(BF)
    for c in range(8):
        at = slice(c * 512, (c + 1) * 512)
        f = dot(fxy, stick_hot[:, at])
        fz = frequency(cells[:, at] // NG)
        kinetic[:, at] = 2.0 * (f[0:1] * f[0:1] + f[1:2] * f[1:2] + fz * fz) / (NG * NG)
    depth_forward = dot_nt(table[1], order).astype(BF)
    rotations("end")

    pltpu.make_async_copy(got2, got2, r2).wait()
    back = got2[...].astype(F32).reshape(ROWS, 2, 8, NG)
    back = jnp.concatenate(
        [back[:, 0].reshape(256, NG), back[:, 1].reshape(256, NG)], axis=1).astype(BF)
    back = dot(depth_forward, back).astype(BF)
    back = jnp.concatenate(
        [
            jnp.concatenate(
                [back[p * NG + u * 64:p * NG + u * 64 + 64, s * NG:(s + 1) * NG] for u in range(2)],
                axis=1)
            for s in range(2) for p in range(2)
        ], axis=0)
    for c in range(8):
        at = slice(c * 512, (c + 1) * 512)
        u = dot(back, stick_hot[:, at])
        hit = lax.broadcasted_iota(jnp.int32, (64, 512), 0) == cells[:, at] // NG % 64
        kin = kinetic[:, at]
        for s in range(2):
            v = jnp.concatenate(
                [jnp.sum(jnp.where(hit, u[(2 * s + p) * 64:(2 * s + p + 1) * 64], 0.0),
                         axis=0, keepdims=True) for p in range(2)], axis=0)
            applied[s, :, at] = v + kin * trial[s, :, at]
    rotations("last")

    for c in range(CUT):
        z_copy(c).wait_recv()
        total = own_part[c] + part_in[c].astype(F32)
        rotated[:, :, c * width:(c + 1) * width] = total.astype(BF).reshape(16, 2, width)

    pltpu.make_async_copy(all_columns.at[pl.ds(0, ROWS - 1)], all_columns.at[pl.ds(0, ROWS - 1)], col_send).wait()
    for sem in (s1, s2):
        pltpu.make_async_copy(got2.at[pl.ds(0, ROWS - 1)], got2.at[pl.ds(0, ROWS - 1)], sem).wait()
    for c in range(CH):
        for d in range(1, XS):
            x_copy(c, d).wait_send()
            if c >= CUT:
                pass_copy(c, d, x).wait_send()
        (z_copy if c < CUT else raw_copy)(c).wait_send()


def local(trial, resident, potential, columns, cells, slab, owner, rotation):
    npw = cells.shape[0]
    width = npw // CH
    vmem = pl.BlockSpec(memory_space=pltpu.VMEM)
    hbm = pl.BlockSpec(memory_space=pl.ANY)
    dma = pltpu.SemaphoreType.DMA
    return pl.pallas_call(
        kernel,
        out_shape=(
            pltpu.VMEM(trial.shape, F32),
            pltpu.VMEM(resident.shape, BF),
        ),
        in_specs=[hbm] * 8,
        out_specs=(vmem, vmem),
        scratch_shapes=[
            pltpu.VMEM(trial.shape, F32),
            pltpu.VMEM(resident.shape, BF),
            pltpu.VMEM(potential.shape, F32),
            pltpu.VMEM((1, NG), jnp.int32),
            pltpu.VMEM((1, npw), jnp.int32),
            pltpu.SMEM((ROWS,), jnp.int32),
            pltpu.SMEM((8,), jnp.int32),
            pltpu.VMEM((16, NG), BF),
            pltpu.VMEM((2, 256, 256), BF),
            dma((8,)),
            pltpu.VMEM((ROWS, 1, NG), jnp.int32),
            pltpu.VMEM((256, npw), BF),
            pltpu.VMEM((256, ROWS * NG), BF),
            pltpu.VMEM((1, npw), F32),
            pltpu.VMEM((ROWS, 16, NG), BF),
            pltpu.VMEM((ROWS, 16, NG), BF),
            pltpu.VMEM((ROWS, 16, NG), BF),
            pltpu.VMEM((ROWS, 16, NG), BF),
            pltpu.VMEM((1024, 256), F32),
            pltpu.VMEM((1024, 256), BF),
            pltpu.VMEM((CH, XS, 32, width), BF),
            pltpu.VMEM((RAW, XS, 32, width), BF),
            pltpu.VMEM((CH, 32, width), F32),
            pltpu.VMEM((CH, 32, width), BF),
            pltpu.VMEM((CH, 32, width), BF),
            pltpu.VMEM((32, NG), BF),
            pltpu.VMEM((32, NG), BF),
            dma, dma, dma, dma((GR,)), dma, dma,
            dma((CH, XS - 1)), dma((CH, XS - 1)), dma((CH,)), dma((CH,)), dma, dma,
            dma((RAW, XS - 1)), dma((RAW, XS - 1)),
        ],
        compiler_params=pltpu.CompilerParams(
            collective_id=0, has_side_effects=True, vmem_limit_bytes=48 * 2**20
        ),
        cost_estimate=pl.CostEstimate(
            flops=4 * 10**9, bytes_accessed=2 * 10**6, transcendentals=0
        ),
    )(*(
        pltpu.with_memory_space_constraint(operand, pltpu.HBM)
        for operand in (
            trial, resident, potential, columns.reshape(1, NG), cells.reshape(1, npw),
            slab, owner, rotation.T,
        )
    ))


def solution(mesh):
    return jax.shard_map(
        local,
        mesh=mesh,
        in_specs=(
            P("col", None, "row"), P("col", None, "row"), P("row", None, None),
            P("row"), P("row"), P(), P(), P(None, "col"),
        ),
        out_specs=(P("col", None, "row"), P("col", None, "row")),
        check_vma=False,
    )
```

```python
import jax
import jax.numpy as jnp
import numpy as np
from jax import lax
from jax.experimental import pallas as pl
from jax.experimental.pallas import tpu as pltpu
from jax.sharding import PartitionSpec as P

NG = 128
ROWS = 32
XS = 4
PAIRS = ROWS // 2
CH = 8
EARLY = 0
LATE = 2
RAW = 2
CUT = CH - RAW
PLAN = {"start": (0, 1), "fill0": (2,), "fill1": (3,), "fill2": (4,), "fill3": (5,), "end": (6, 7)}
PASS = {"fill1": (6,), "fill3": (7,)}
GR = 4
MESH = pl.DeviceIdType.MESH
F32 = jnp.float32
BF = jnp.bfloat16
NT = (((1,), (1,)), ((), ()))


def dot(a, b):
    return jnp.dot(a, b, preferred_element_type=F32)


def dot_nt(a, b):
    return lax.dot_general(a, b, NT, preferred_element_type=F32)


def onehot(key, size):
    rows = lax.broadcasted_iota(jnp.int32, (size, key.shape[-1]), 0)
    return jnp.where(rows == key, 1.0, 0.0).astype(BF)


def frequency(j):
    return jnp.where(j < NG // 2, j, j - NG).astype(F32)


def make_table(table):
    a = lax.broadcasted_iota(jnp.int32, (NG, NG), 0)
    b = lax.broadcasted_iota(jnp.int32, (NG, NG), 1)
    step = lax.broadcasted_iota(jnp.int32, (8, NG), 1).astype(F32)
    wave = jnp.tile(jnp.cos(step * (2.0 * np.pi / NG)), (NG // 8, 1))
    k = a * b
    c = jnp.take_along_axis(wave, k % NG, axis=1)
    s = jnp.take_along_axis(wave, (k + 3 * NG // 4) % NG, axis=1)
    top = jnp.concatenate([c, -s], axis=1)
    flip = jnp.concatenate([c, s], axis=1)
    low = jnp.concatenate([s, c], axis=1)
    table[0] = jnp.concatenate([top, low], axis=0).astype(BF)
    low = jnp.concatenate([-s, c], axis=1)
    table[1] = jnp.concatenate([flip, low], axis=0).astype(BF)


def kernel(
    trial_in, resident_in, potential_in, columns_in, cells_in, slab_in, owner_in, rotation_in,
    applied, rotated,
    trial, resident, potential, columns, cells, slab, owner, rotation, table, loads,
    all_columns, stick_hot, plane_hot, kinetic, sent1, got1, sent2, got2,
    grid, picked, panels, others, own_part, part_out, part_in, weight_out, weight_in,
    col_send, col_recv, s1, r1, s2, r2, xs, xr, zs, zr, ws, wr, fs, fr,
):
    col = lax.axis_index("col")
    row = lax.axis_index("row")
    half = col // XS
    x = lax.rem(col, XS)
    mate = lax.rem(col + XS, 2 * XS)
    pair = row // 2
    core = lax.rem(row, 2)
    sibling = row + 1 - 2 * core
    npw = cells_in.shape[-1]
    width = npw // CH

    def x_peer(d):
        return half * XS + lax.rem(x + d, XS)

    def peer(q, i):
        return lax.rem(pair + q, PAIRS) * 2 + i

    def slot(q):
        return lax.rem(PAIRS - q, PAIRS) * 2 + core

    load = [
        pltpu.make_async_copy(source, target, loads.at[i])
        for i, (source, target) in enumerate((
            (columns_in, columns), (cells_in, cells), (resident_in, resident),
            (rotation_in, rotation), (trial_in, trial), (potential_in, potential),
            (slab_in, slab), (owner_in, owner),
        ))
    ]
    for i in (1, 4, 2, 0, 6, 3, 7, 5):
        load[i].start()

    barrier = pltpu.get_barrier_semaphore()

    def greet(d, carry):
        pl.semaphore_signal(
            barrier, inc=1, device_id=(col, lax.rem(row + d, ROWS)), device_id_type=MESH
        )
        return carry

    lax.fori_loop(1, ROWS, greet, 0)
    for d in range(1, XS):
        pl.semaphore_signal(barrier, inc=1, device_id=(x_peer(d), row), device_id_type=MESH)
    pl.semaphore_signal(barrier, inc=1, device_id=(mate, row), device_id_type=MESH)

    make_table(table)

    load[1].wait()
    load[4].wait()

    def stick_part(c):
        at = slice(c * 512, (c + 1) * 512)
        cell = cells[:, at]
        z = cell // NG
        hot = onehot((z // 64) * NG + cell % NG, 256)
        stick_hot[:, at] = hot
        deep = onehot(z % 64, 64)
        left = jnp.concatenate(
            [deep * trial[s, p:p + 1, at].astype(BF) for s in range(2) for p in range(2)], axis=0
        )
        return dot_nt(left, hot)

    def sticks(first, last, acc=None):
        for c in range(first, last):
            acc = stick_part(c) if acc is None else acc + stick_part(c)
        return acc

    filled = sticks(0, EARLY) if EARLY else None

    load[2].wait()
    for c in range(CH):
        block = resident[:, :, c * width:(c + 1) * width].reshape(32, width)
        panels[c, pl.ds(x, 1)] = block[None]
    load[0].wait()
    all_columns[pl.ds(core, 1)] = columns[...].reshape(1, 1, NG)

    load[3].wait()
    load[7].wait()
    lane = lax.broadcasted_iota(jnp.int32, (16, NG), 1)
    sub = lax.broadcasted_iota(jnp.int32, (16, NG), 0)
    perm = jnp.concatenate(
        [jnp.where(lane == owner[p] * 16 + sub, 1.0, 0.0) for p in range(8)], axis=0
    ).astype(BF)
    by_group = dot(rotation[...], perm).astype(BF)
    up = jnp.where(
        lax.broadcasted_iota(jnp.int32, (32, 16), 0) // 2
        == lax.broadcasted_iota(jnp.int32, (32, 16), 1), 1.0, 0.0).astype(BF)
    out = jnp.where(
        lax.broadcasted_iota(jnp.int32, (NG, 256), 1) // 2
        == lax.broadcasted_iota(jnp.int32, (NG, 256), 0), 1.0, 0.0).astype(BF)
    spread = dot(dot(up, by_group).astype(BF), out)
    same = (
        lax.broadcasted_iota(jnp.int32, (32, 256), 0) % 2
        == lax.broadcasted_iota(jnp.int32, (32, 256), 1) % 2
    )
    spread = jnp.where(same, spread, 0.0)
    weight_own = jnp.where(half == 0, spread[:, :NG], spread[:, NG:]).astype(BF)
    weight_out[...] = jnp.where(half == 0, spread[:, NG:], spread[:, :NG]).astype(BF)
    pl.semaphore_wait(barrier, ROWS - 1 + XS - 1 + 1)

    w_copy = pltpu.make_async_remote_copy(
        weight_out, weight_in, ws, wr, device_id=(mate, row), device_id_type=MESH
    )
    w_copy.start()

    def x_copy(c, d):
        return pltpu.make_async_remote_copy(
            panels.at[c, x], panels.at[c, x], xs.at[c, d - 1], xr.at[c, d - 1],
            device_id=(x_peer(d), row), device_id_type=MESH,
        )

    def x_arrival(c, d):
        return pltpu.make_async_remote_copy(
            panels.at[c, x], panels.at[c, lax.rem(x + XS - d, XS)], xs.at[c, d - 1], xr.at[c, d - 1],
            device_id=(x_peer(d), row), device_id_type=MESH,
        )

    def rotate(c):
        if c == 0:
            w_copy.wait()
        for d in range(1, XS):
            x_arrival(c, d).wait_recv()
        both = jnp.concatenate([weight_own, weight_in[...]], axis=0)
        r = dot(both, panels[c].reshape(4 * 32, width))
        own_part[c] = r[:32]
        part_out[c] = r[32:].astype(BF)
        z_copy(c).start()

    def raw_copy(c):
        return pltpu.make_async_remote_copy(
            panels.at[c, x], others.at[c - CUT, x], zs.at[c], zr.at[c],
            device_id=(mate, row), device_id_type=MESH,
        )

    def pass_copy(c, d, at):
        return pltpu.make_async_remote_copy(
            others.at[c - CUT, x], others.at[c - CUT, at], fs.at[c - CUT, d - 1], fr.at[c - CUT, d - 1],
            device_id=(x_peer(d), row), device_id_type=MESH,
        )

    def pass_on(c):
        raw_copy(c).wait_recv()
        for d in (2, 1, 3):
            pass_copy(c, d, x).start()

    def rotate_raw(c):
        for d in range(1, XS):
            x_arrival(c, d).wait_recv()
            pass_copy(c, d, lax.rem(x + XS - d, XS)).wait_recv()
        r = dot(weight_own, panels[c].reshape(4 * 32, width))
        r = r + dot(weight_out[...], others[c - CUT].reshape(4 * 32, width))
        rotated[:, :, c * width:(c + 1) * width] = r.astype(BF).reshape(16, 2, width)

    def z_copy(c):
        return pltpu.make_async_remote_copy(
            part_out.at[c], part_in.at[c], zs.at[c], zr.at[c],
            device_id=(mate, row), device_id_type=MESH,
        )

    def rotations(place):
        for c in PASS.get(place, ()):
            pass_on(c)
        for c in PLAN.get(place, ()):
            (rotate if c < CUT else rotate_raw)(c)

    def send_column(q, i, to):
        pltpu.make_async_remote_copy(
            columns, all_columns.at[slot(q)], col_send, col_recv,
            device_id=(col, to), device_id_type=MESH,
        ).start()

    for c in range(CUT, CH):
        raw_copy(c).start()
    for d in (2, 1, 3):
        x_copy(0, d).start()
    send_column(0, 0, sibling)

    def send_columns(q, carry):
        send_column(q, 0, peer(q, 0))
        send_column(q, 1, peer(q, 1))
        return carry

    lax.fori_loop(1, PAIRS, send_columns, 0)
    for c in range(1, LATE):
        for d in (2, 1, 3):
            x_copy(c, d).start()

    filled = sticks(EARLY, 8, filled)
    filled = jnp.concatenate(
        [
            jnp.concatenate(
                [filled[(2 * s + p) * 64:(2 * s + p + 1) * 64, u * NG:(u + 1) * NG]
                 for p in range(2) for u in range(2)], axis=0)
            for s in range(2)
        ], axis=1).astype(BF)

    load[6].wait()
    j = lax.broadcasted_iota(jnp.int32, (8, 256), 0)
    k = lax.broadcasted_iota(jnp.int32, (8, 256), 1)
    want = j // 4 * NG + j % 4
    order = jnp.concatenate(
        [jnp.where(k == want + slab[r] * 4, 1.0, 0.0) for r in range(ROWS)], axis=0
    ).astype(BF)
    depth_inverse = dot(order, table[0]).astype(BF)
    spread_z = dot(depth_inverse, filled)
    for r in range(ROWS):
        rows = slice(8 * r, 8 * r + 8)
        sent1[r] = jnp.concatenate([spread_z[rows, :NG], spread_z[rows, NG:]], axis=0).astype(BF)

    def send_stick(q, to):
        at = slot(q)
        pltpu.make_async_remote_copy(
            sent1.at[to], got1.at[at], s1, r1.at[at // (ROWS // GR)],
            device_id=(col, to), device_id_type=MESH,
        ).start()

    send_stick(0, sibling)

    def send_sticks(n, carry):
        q = PAIRS - n
        send_stick(q, peer(q, 0))
        send_stick(q, peer(q, 1))
        return carry

    lax.fori_loop(1, PAIRS, send_sticks, 0)
    pltpu.make_async_copy(sent1.at[row], got1.at[core], r1.at[0]).start()
    for c in range(LATE, CH):
        for d in (2, 1, 3):
            x_copy(c, d).start()
    rotations("sent")


    pltpu.make_async_copy(all_columns.at[pl.ds(0, ROWS - 1)], all_columns.at[pl.ds(0, ROWS - 1)], col_recv).wait()
    for c in range(8):
        key = jnp.concatenate([all_columns[4 * c + i] for i in range(4)], axis=1)
        plane_hot[:, c * 512:(c + 1) * 512] = onehot(key // (64 * NG) * NG + key % NG, 256)

    rotations("start")

    per = ROWS // GR
    for g in range(GR):
        pltpu.make_async_copy(got1.at[pl.ds(g * per, per)], got1.at[pl.ds(g * per, per)], r1.at[g]).wait()
        key = jnp.concatenate([all_columns[per * g + i] for i in range(per)], axis=1)
        across = onehot(key // NG % 64, 64)
        values = jnp.concatenate([got1[per * g + i] for i in range(per)], axis=1)
        right = plane_hot[:, g * per * NG:(g + 1) * per * NG]
        for m in range(4):
            left = jnp.concatenate(
                [across * values[4 * m + i:4 * m + i + 1] for i in range(4)], axis=0
            )
            part = dot_nt(left, right)
            if g == 0:
                grid[256 * m:256 * m + 256] = part
            else:
                grid[256 * m:256 * m + 256] += part
        rotations("fill%d" % g)

    load[5].wait()
    level = jnp.concatenate([potential[q] for q in range(4)], axis=0) * (2.0 ** -21)
    level = jnp.concatenate([level, level], axis=1)
    for s in range(2):
        t = jnp.concatenate(
            [
                jnp.concatenate(
                    [grid[i * 64:(i + 1) * 64, u * NG:(u + 1) * NG]
                     for i in (8 * s + q, 8 * s + 4 + q) for u in range(2)], axis=0)
                for q in range(4)
            ], axis=1).astype(BF)
        t = dot(table[0], t).astype(BF)
        t = jnp.concatenate(
            [jnp.concatenate([t[:NG, q * NG:(q + 1) * NG], t[NG:, q * NG:(q + 1) * NG]], axis=1)
             for q in range(4)], axis=0)
        t = dot(t, table[1])
        t = (t * level).astype(BF)
        t = dot(t, table[0]).astype(BF)
        t = jnp.concatenate(
            [jnp.concatenate([t[q * NG:(q + 1) * NG, :NG], t[q * NG:(q + 1) * NG, NG:]], axis=0)
             for q in range(4)], axis=1)
        t = dot(table[1], t).astype(BF)
        for q in range(4):
            for p in range(2):
                picked[((2 * s + p) * 4 + q) * 64:((2 * s + p) * 4 + q + 1) * 64] = jnp.concatenate(
                    [t[p * NG + u * 64:p * NG + u * 64 + 64, q * NG:(q + 1) * NG] for u in range(2)],
                    axis=1)
        rotations("plane%d" % s)

    for q in range(PAIRS):
        u = dot(picked[...], plane_hot[:, q * 256:q * 256 + 256])
        key = jnp.concatenate([all_columns[2 * q], all_columns[2 * q + 1]], axis=1)
        hit = lax.broadcasted_iota(jnp.int32, (64, 256), 0) == key // NG % 64
        got = jnp.concatenate(
            [jnp.sum(jnp.where(hit, u[i * 64:(i + 1) * 64], 0.0), axis=0, keepdims=True)
             for i in range(16)], axis=0).astype(BF)
        for i in range(2):
            sent2[2 * q + i] = got[:, i * NG:(i + 1) * NG]
        for i in range(2) if q else (0,):
            pltpu.make_async_remote_copy(
                sent2.at[2 * q + i] if q else sent2.at[1 - core], got2.at[row], s2, r2,
                device_id=(col, peer(q, i) if q else sibling), device_id_type=MESH,
            ).start()
        rotations("pick%d" % q)
    pltpu.make_async_copy(sent2.at[core], got2.at[row], r2).start()

    own_col = columns[...]
    fx, fy = frequency(own_col // NG), frequency(own_col % NG)
    rows16 = lax.broadcasted_iota(jnp.int32, (16, NG), 0)
    fxy = jnp.where(rows16 == 0, fx, jnp.where(rows16 == 1, fy, 0.0))
    fxy = jnp.concatenate([fxy, fxy], axis=1).astype(BF)
    for c in range(8):
        at = slice(c * 512, (c + 1) * 512)
        f = dot(fxy, stick_hot[:, at])
        fz = frequency(cells[:, at] // NG)
        kinetic[:, at] = 2.0 * (f[0:1] * f[0:1] + f[1:2] * f[1:2] + fz * fz) / (NG * NG)
    depth_forward = dot_nt(table[1], order).astype(BF)
    rotations("end")

    pltpu.make_async_copy(got2, got2, r2).wait()
    back = got2[...].astype(F32).reshape(ROWS, 2, 8, NG)
    back = jnp.concatenate(
        [back[:, 0].reshape(256, NG), back[:, 1].reshape(256, NG)], axis=1).astype(BF)
    back = dot(depth_forward, back).astype(BF)
    back = jnp.concatenate(
        [
            jnp.concatenate(
                [back[p * NG + u * 64:p * NG + u * 64 + 64, s * NG:(s + 1) * NG] for u in range(2)],
                axis=1)
            for s in range(2) for p in range(2)
        ], axis=0)
    for c in range(8):
        at = slice(c * 512, (c + 1) * 512)
        u = dot(back, stick_hot[:, at])
        hit = lax.broadcasted_iota(jnp.int32, (64, 512), 0) == cells[:, at] // NG % 64
        kin = kinetic[:, at]
        for s in range(2):
            v = jnp.concatenate(
                [jnp.sum(jnp.where(hit, u[(2 * s + p) * 64:(2 * s + p + 1) * 64], 0.0),
                         axis=0, keepdims=True) for p in range(2)], axis=0)
            applied[s, :, at] = v + kin * trial[s, :, at]
    rotations("last")

    for c in range(CUT):
        z_copy(c).wait_recv()
        total = own_part[c] + part_in[c].astype(F32)
        rotated[:, :, c * width:(c + 1) * width] = total.astype(BF).reshape(16, 2, width)

    pltpu.make_async_copy(all_columns.at[pl.ds(0, ROWS - 1)], all_columns.at[pl.ds(0, ROWS - 1)], col_send).wait()
    for sem in (s1, s2):
        pltpu.make_async_copy(got2.at[pl.ds(0, ROWS - 1)], got2.at[pl.ds(0, ROWS - 1)], sem).wait()
    for c in range(CH):
        for d in range(1, XS):
            x_copy(c, d).wait_send()
            if c >= CUT:
                pass_copy(c, d, x).wait_send()
        (z_copy if c < CUT else raw_copy)(c).wait_send()


def local(trial, resident, potential, columns, cells, slab, owner, rotation):
    npw = cells.shape[0]
    width = npw // CH
    vmem = pl.BlockSpec(memory_space=pltpu.VMEM)
    hbm = pl.BlockSpec(memory_space=pl.ANY)
    dma = pltpu.SemaphoreType.DMA
    return pl.pallas_call(
        kernel,
        out_shape=(
            pltpu.VMEM(trial.shape, F32),
            pltpu.VMEM(resident.shape, BF),
        ),
        in_specs=[hbm] * 8,
        out_specs=(vmem, vmem),
        scratch_shapes=[
            pltpu.VMEM(trial.shape, F32),
            pltpu.VMEM(resident.shape, BF),
            pltpu.VMEM(potential.shape, F32),
            pltpu.VMEM((1, NG), jnp.int32),
            pltpu.VMEM((1, npw), jnp.int32),
            pltpu.SMEM((ROWS,), jnp.int32),
            pltpu.SMEM((8,), jnp.int32),
            pltpu.VMEM((16, NG), BF),
            pltpu.VMEM((2, 256, 256), BF),
            dma((8,)),
            pltpu.VMEM((ROWS, 1, NG), jnp.int32),
            pltpu.VMEM((256, npw), BF),
            pltpu.VMEM((256, ROWS * NG), BF),
            pltpu.VMEM((1, npw), F32),
            pltpu.VMEM((ROWS, 16, NG), BF),
            pltpu.VMEM((ROWS, 16, NG), BF),
            pltpu.VMEM((ROWS, 16, NG), BF),
            pltpu.VMEM((ROWS, 16, NG), BF),
            pltpu.VMEM((1024, 256), F32),
            pltpu.VMEM((1024, 256), BF),
            pltpu.VMEM((CH, XS, 32, width), BF),
            pltpu.VMEM((RAW, XS, 32, width), BF),
            pltpu.VMEM((CH, 32, width), F32),
            pltpu.VMEM((CH, 32, width), BF),
            pltpu.VMEM((CH, 32, width), BF),
            pltpu.VMEM((32, NG), BF),
            pltpu.VMEM((32, NG), BF),
            dma, dma, dma, dma((GR,)), dma, dma,
            dma((CH, XS - 1)), dma((CH, XS - 1)), dma((CH,)), dma((CH,)), dma, dma,
            dma((RAW, XS - 1)), dma((RAW, XS - 1)),
        ],
        compiler_params=pltpu.CompilerParams(
            collective_id=0, has_side_effects=True, vmem_limit_bytes=48 * 2**20
        ),
        cost_estimate=pl.CostEstimate(
            flops=4 * 10**9, bytes_accessed=2 * 10**6, transcendentals=0
        ),
    )(*(
        pltpu.with_memory_space_constraint(operand, pltpu.HBM)
        for operand in (
            trial, resident, potential, columns.reshape(1, NG), cells.reshape(1, npw),
            slab, owner, rotation.T,
        )
    ))


def solution(mesh):
    return jax.shard_map(
        local,
        mesh=mesh,
        in_specs=(
            P("col", None, "row"), P("col", None, "row"), P("row", None, None),
            P("row"), P("row"), P(), P(), P(None, "col"),
        ),
        out_specs=(P("col", None, "row"), P("col", None, "row")),
        check_vma=False,
    )
```
